32 devices in a mesh: grp: 2 (over y), lat: 8 (over z, x), row: 2 (over core).
Axes of the slice: x: 2, y: 2, z: 4, core: 2. Of those that a mesh axis runs over, the one named last changes fastest.
Arguments:
- activations: bfloat16 [32, 128, 4096], P(('grp', 'row'), 'lat'), parts along dimension 0, may hold values from -6 to 6
- act_blocks: int32 [32, 4], P('grp'), parts along dimension 0, may hold values from -1 to 7, as said below
- dictionary: bfloat16 [4096, 4096], P(('grp', 'lat', 'row')), parts along dimension 0, may hold values from -0.09375 to 0.09375
- enc_bias: bfloat16 [4096], P(('grp', 'lat', 'row')), parts along dimension 0, may hold values from -1 to 1
- dec_bias: bfloat16 [8192], P('grp'), parts along dimension 0, may hold values from -3 to 3
Outputs:
- dict_grad: bfloat16 [4096, 4096], P(('grp', 'lat', 'row')), parts along dimension 0
The draws below stay inside these ranges and needn't reach their ends.
There are 2 independent parts, one for each index of `grp`. The reference program is written for one: setup_inputs(seed, part) draws one part's arguments, and reference() takes and returns one part's arrays. A program takes and returns all parts, laid end to end along the dimension named above; each array names one. Nothing has to cross between parts.
Inputs may be any that keep to these rules, and one draw needn't show every extreme that they name: `act_blocks`: each row lists 1 to 4 distinct latent blocks first and -1 after them. Among the row blocks of either half (the first 8 and the rest) no latent block is listed by more than 4 of them, and in every draw some latent block is listed by exactly 4 row blocks of one half.
All inputs are finite; a program needn't handle non-finite values.
Results may differ from the reference program's by a relative error of at most 0.005.
Values may be sent and summed in bfloat16 or wider, within the bound.
No kernel may reach another device: no remote copies, remote signals or barrier semaphores. Data moves between devices by JAX's collectives and lax.ppermute only.
A program may use at most 128 MiB of HBM per device.

```python
import jax
import jax.numpy as jnp
from jax import lax

D = 4096
LB = 256
RB = 128
KMAX = 4
LAT = 2048
NBLK = 16
CAP = 4
N_LAT = 8
N_ROW = 2


def draw_act_blocks(key, part):
    key = jax.random.fold_in(key, 17)
    keys = jax.random.split(key, 5)
    half_blocks = NBLK // N_ROW
    labels = jax.random.permutation(keys[0], N_LAT).astype(jnp.int32)
    first_draw = jax.random.randint(keys[1], (NBLK,), 1, KMAX + 1)
    second_draw = jax.random.randint(keys[2], (NBLK,), 1, KMAX + 1)
    counts = jnp.minimum(first_draw, second_draw)
    busy_half = jax.random.randint(keys[3], (), 0, N_ROW)
    busy_place = jax.random.randint(keys[4], (), 0, N_LAT)
    row_ids = jnp.arange(NBLK, dtype=jnp.int32)
    local_row = row_ids % half_blocks
    cycle_pos = local_row % N_LAT
    ahead = (busy_place - cycle_pos) % N_LAT
    forced = (row_ids // half_blocks == busy_half) & (ahead < KMAX)
    counts = jnp.where(forced, KMAX, counts)
    places = jnp.arange(KMAX, dtype=jnp.int32)
    names = labels[(cycle_pos[:, None] + places[None, :]) % N_LAT]
    return jnp.where(places[None, :] < counts[:, None], names, -1).astype(jnp.int32)


def block_levels(rng, extent, cuts, smallest, high):
    gain = 1.0
    for dim, parts in cuts:
        steps = jax.random.uniform(jax.random.fold_in(jax.random.fold_in(rng, 6), dim), (parts,), jnp.float32, smallest / len(cuts), high / len(cuts))
        gain = gain * jnp.repeat(jnp.exp(steps), extent[dim] // parts).reshape((-1,) + (1,) * (len(extent) - 1 - dim))
    return gain


def scatter_about(own_key, extent, deviation, bound, cuts=(), kind=jnp.bfloat16):
    drawn = deviation * jax.random.normal(own_key, extent, jnp.float32)
    if cuts:
        drawn = drawn * block_levels(own_key, extent, cuts, -0.22, 0.18)
    return jnp.clip(drawn, -bound, bound).astype(kind)


def setup_inputs(seed: int = 0, part: int = 0) -> dict:
    key_of = jax.random.split(jax.random.key(seed), 6)
    own_keys = jax.random.split(jax.random.fold_in(key_of[5], part), 6)
    return {
        "activations": scatter_about(own_keys[0], (NBLK, RB, D), 1.0, 6.0, ((0, 2), (1, 8))),
        "act_blocks": draw_act_blocks(jax.random.fold_in(jax.random.fold_in(key_of[5], part), 71), part),
        "dictionary": scatter_about(own_keys[2], (LAT, D), D ** -0.5, 0.09375, ((0, 16),)),
        "enc_bias": jnp.clip(jax.random.uniform(own_keys[3], (LAT,), jnp.float32, -1.0, 1.0) * block_levels(own_keys[3], (LAT,), ((0, 16),), -0.4, 0.0), -1.0, 1.0).astype(jnp.bfloat16),
        "dec_bias": scatter_about(own_keys[4], (D,), 0.5, 3.0),
    }


def slot_tables(lists, block_count, slot_count):
    row_total = lists.shape[0]
    labels = jnp.arange(block_count, dtype=jnp.int32)
    matches = jnp.sum((lists[:, :, None] == labels[None, None, :]).astype(jnp.int32), axis=1)
    position = jnp.cumsum(matches, axis=0) - 1
    places = jnp.arange(slot_count, dtype=jnp.int32)
    hits = ((matches[:, :, None] == 1) & (position[:, :, None] == places[None, None, :])).astype(jnp.int32)
    row_ids = jnp.arange(row_total, dtype=jnp.int32)
    table = jnp.sum(hits * row_ids[:, None, None], axis=0).astype(jnp.int32)
    filled = jnp.sum(hits, axis=0).astype(jnp.int32)
    return table, filled


def reference(activations, act_blocks, dictionary, enc_bias, dec_bias):
    half_blocks = NBLK // N_ROW
    centred = (activations.astype(jnp.float32) - dec_bias.astype(jnp.float32)).astype(jnp.bfloat16)
    lists = act_blocks.reshape(N_ROW, half_blocks, KMAX)
    tables, filled = jax.vmap(lambda part_lists: slot_tables(part_lists, N_LAT, CAP))(lists)
    offsets = (jnp.arange(N_ROW, dtype=jnp.int32) * half_blocks)[:, None, None]
    where_rows = jnp.transpose(tables + offsets, (1, 0, 2)).reshape(N_LAT, N_ROW * CAP).astype(jnp.int32)
    slot_mask = jnp.transpose(filled, (1, 0, 2)).reshape(N_LAT, N_ROW * CAP).astype(jnp.float32)
    blocks = dictionary.reshape(N_LAT, LB, D)
    biases = enc_bias.reshape(N_LAT, LB)

    def forward(rebuilt, inputs):
        where, weight_mask, block, bias = inputs
        slot_rows = centred[where].astype(jnp.float32)
        block_f = block.astype(jnp.float32)
        preacts = jnp.einsum('srd,ld->srl', slot_rows, block_f) + bias.astype(jnp.float32)
        latent_codes = jax.nn.softplus(preacts).astype(jnp.bfloat16)
        pieces = jnp.einsum('srl,ld->srd', latent_codes.astype(jnp.float32), block_f).astype(jnp.bfloat16)
        rebuilt = rebuilt.at[where].add(pieces.astype(jnp.float32) * weight_mask[:, None, None])
        return rebuilt, (latent_codes, jax.nn.sigmoid(preacts))

    rebuilt, (all_codes, all_sigmas) = lax.scan(
        forward, jnp.zeros((NBLK, RB, D), jnp.float32), (where_rows, slot_mask, blocks, biases))
    errors = (rebuilt - centred.astype(jnp.float32)).astype(jnp.bfloat16)

    def backward(inputs):
        where, weight_mask, block, latent_codes, sigmas = inputs
        slot_rows = centred[where].astype(jnp.float32)
        err_rows = errors[where].astype(jnp.float32) * weight_mask[:, None, None]
        code_grads = jnp.einsum('srd,ld->srl', err_rows, block.astype(jnp.float32))
        slopes = (code_grads * sigmas).astype(jnp.bfloat16)
        masked_codes = latent_codes.astype(jnp.float32) * weight_mask[:, None, None]
        total = jnp.einsum('srl,srd->ld', masked_codes, err_rows)
        total = total + jnp.einsum('srl,srd->ld', slopes.astype(jnp.float32), slot_rows)
        return (total / RB).astype(jnp.bfloat16)

    grads = lax.map(backward, (where_rows, slot_mask, blocks, all_codes, all_sigmas))
    return grads.reshape(LAT, D)
```

```python
from functools import partial

import jax
import jax.numpy as jnp
from jax import lax
from jax.sharding import PartitionSpec as P

GATHER_LIMIT = 32 * 2**20


def slot_tables(lists, block_count, slot_count):
    row_total = lists.shape[0]
    labels = jnp.arange(block_count, dtype=jnp.int32)
    matches = jnp.sum((lists[:, :, None] == labels[None, None, :]).astype(jnp.int32), axis=1)
    position = jnp.cumsum(matches, axis=0) - 1
    places = jnp.arange(slot_count, dtype=jnp.int32)
    hits = ((matches[:, :, None] == 1) & (position[:, :, None] == places[None, None, :])).astype(
        jnp.int32
    )
    row_ids = jnp.arange(row_total, dtype=jnp.int32)
    table = jnp.sum(hits * row_ids[:, None, None], axis=0)
    filled = jnp.sum(hits, axis=0)
    return (table, filled)


def encode_slot(dict_full, bias_full, slot_rows, is_filled):
    latent_width = dict_full.shape[0]

    def encode_active(inputs):
        preacts = jnp.einsum("rd,ld->rl", inputs, dict_full, preferred_element_type=jnp.float32)
        preacts = preacts + bias_full.astype(jnp.float32)
        latent_codes = jax.nn.softplus(preacts).astype(jnp.bfloat16)
        pieces = jnp.einsum(
            "rl,ld->rd", latent_codes, dict_full, preferred_element_type=jnp.float32
        )
        return (latent_codes, jax.nn.sigmoid(preacts), pieces.astype(jnp.bfloat16))

    def encode_vacant(inputs):
        return (
            jnp.zeros((inputs.shape[0], latent_width), jnp.bfloat16),
            jnp.zeros((inputs.shape[0], latent_width), jnp.float32),
            jnp.zeros_like(inputs),
        )

    return lax.cond(is_filled > 0, encode_active, encode_vacant, slot_rows)


def slope_slot(dict_full, err_rows, sigmas, is_filled):

    def slope_active(err_in, sig_in):
        code_grads = jnp.einsum("rd,ld->rl", err_in, dict_full, preferred_element_type=jnp.float32)
        return (code_grads * sig_in).astype(jnp.bfloat16)

    def slope_vacant(err_in, sig_in):
        return jnp.zeros(sig_in.shape, jnp.bfloat16)

    return lax.cond(is_filled > 0, slope_active, slope_vacant, err_rows, sigmas)


def exchange_body(activations, act_blocks, dictionary, enc_bias, dec_bias):
    lat_count = lax.axis_size("lat")
    row_count = lax.axis_size("row")
    lat_index = lax.axis_index("lat")
    row_index = lax.axis_index("row")
    half_blocks, rows_each, feature_dim = activations.shape
    list_width = act_blocks.shape[1]
    slot_count = list_width * half_blocks // lat_count
    block_rows = rows_each * lat_count
    flat_width = rows_each * feature_dim
    dict_full, bias_full = (
        lax.all_gather(dictionary, "row", axis=0, tiled=True),
        lax.all_gather(enc_bias, "row", axis=0, tiled=True),
    )
    flat_acts = activations.reshape(half_blocks, flat_width)
    bias_flat = jnp.tile(dec_bias.astype(jnp.float32), rows_each)
    centred = (flat_acts.astype(jnp.float32) - bias_flat[None, :]).astype(jnp.bfloat16)
    lists = act_blocks.reshape(row_count, half_blocks, list_width)
    tables, filled = jax.vmap(partial(slot_tables, block_count=lat_count, slot_count=slot_count))(
        lists
    )
    own_table = lax.dynamic_index_in_dim(tables, row_index, 0, keepdims=False)
    own_filled = lax.dynamic_index_in_dim(filled, row_index, 0, keepdims=False)
    mine_filled = lax.dynamic_index_in_dim(filled, lat_index, 1, keepdims=False)
    send_rows = own_table.T
    send_live = own_filled.T
    slot_flags = lax.dynamic_index_in_dim(mine_filled, row_index, 0, keepdims=False)
    wire_shape = (slot_count, block_rows, feature_dim)
    mask_bf = send_live.astype(jnp.bfloat16)[..., None]
    mask_f = send_live.astype(jnp.float32)[..., None]
    back_shape = send_rows.shape + (flat_width,)
    outgoing = (centred[send_rows] * mask_bf).reshape(wire_shape)
    items = lax.all_to_all(outgoing, "lat", split_axis=1, concat_axis=1, tiled=True)
    latent_codes, sigmas, pieces = lax.map(
        lambda bundle: encode_slot(dict_full, bias_full, bundle[0], bundle[1]), (items, slot_flags)
    )
    returned = lax.all_to_all(pieces, "lat", split_axis=1, concat_axis=1, tiled=True)
    returned = returned.reshape(back_shape).astype(jnp.float32) * mask_f
    rebuilt = jnp.zeros((half_blocks, flat_width), jnp.float32).at[send_rows].add(returned)
    errors = (rebuilt - centred.astype(jnp.float32)).astype(jnp.bfloat16)
    err_out = (errors[send_rows] * mask_bf).reshape(wire_shape)
    err_items = lax.all_to_all(err_out, "lat", split_axis=1, concat_axis=1, tiled=True)
    slopes = lax.map(
        lambda bundle: slope_slot(dict_full, bundle[0], bundle[1], bundle[2]),
        (err_items, sigmas, slot_flags),
    )
    total = jnp.einsum("srl,srd->ld", latent_codes, err_items, preferred_element_type=jnp.float32)
    total = total + jnp.einsum("srl,srd->ld", slopes, items, preferred_element_type=jnp.float32)
    grads = lax.psum_scatter(total / block_rows, "row", scatter_dimension=0, tiled=True)
    return grads.astype(jnp.bfloat16)


def ring_body(activations, act_blocks, dictionary, enc_bias, dec_bias):
    count = lax.axis_size("lat")
    lat_index = lax.axis_index("lat")
    row_index = lax.axis_index("row")
    half_blocks, rows_each, width = activations.shape
    latents = dictionary.shape[0]
    cut = latents // 2
    block_rows = rows_each * count
    half = count // 2

    order = list(range(0, count, 2)) + list(range(count - 1, 0, -2))
    place_of = [order.index(i) for i in range(count)]
    order_table = jnp.array(order, jnp.int32)
    place = jnp.array(place_of, jnp.int32)[lat_index]
    right_pairs = [(order[i], order[(i + 1) % count]) for i in range(count)]
    left_pairs = [(b, a) for a, b in right_pairs]

    def to_right(x):
        return lax.ppermute(x, "lat", right_pairs)

    def to_left(x):
        return lax.ppermute(x, "lat", left_pairs)

    def to_core(x):
        return lax.ppermute(x, "row", [(0, 1), (1, 0)])

    def owner(step):
        return order_table[(place + step) % count]

    words = {0: dictionary}
    for step in range(1, half):
        words[-step] = to_right(words[1 - step])
        words[step] = to_left(words[step - 1])
    words[half] = jnp.concatenate([to_right(words[1 - half][:cut]), to_left(words[half - 1][cut:])])

    centred = (activations.astype(jnp.float32) - dec_bias.astype(jnp.float32)).astype(jnp.bfloat16)
    centred = centred.reshape(half_blocks * rows_each, width)
    rows = jnp.concatenate([centred, to_core(centred)])
    biases = lax.all_gather(enc_bias, "lat", axis=0).astype(jnp.float32)
    lists = act_blocks.reshape(2, half_blocks, act_blocks.shape[1])
    lists = jnp.where(row_index == 0, lists, lists[::-1]).reshape(2 * half_blocks, -1)

    steps = [0] + [s for t in range(1, half) for s in (-t, t)] + [half]
    codes, sigmas = {}, {}
    rebuilt = None
    for step in steps:
        block = owner(step)
        bias = lax.dynamic_index_in_dim(biases, block, 0, keepdims=False)
        listed = jnp.repeat(jnp.any(lists == block, axis=1), rows_each)[:, None]
        preacts = jnp.einsum("rd,ld->rl", rows, words[step], preferred_element_type=jnp.float32)
        preacts = preacts + bias
        codes[step] = jnp.where(listed, jax.nn.softplus(preacts), 0.0).astype(jnp.bfloat16)
        sigmas[step] = jnp.where(listed, jax.nn.sigmoid(preacts), 0.0)
        pieces = jnp.einsum(
            "rl,ld->rd", codes[step], words[step], preferred_element_type=jnp.float32
        )
        rebuilt = pieces if rebuilt is None else rebuilt + pieces
    rebuilt = rebuilt.astype(jnp.bfloat16)
    swapped = to_core(rebuilt)
    middle = half_blocks * rows_each
    swapped = jnp.concatenate([swapped[middle:], swapped[:middle]])
    errors = rebuilt.astype(jnp.float32) + swapped.astype(jnp.float32) - rows.astype(jnp.float32)
    errors = errors.astype(jnp.bfloat16)

    def grads_of(step):
        slopes = jnp.einsum("rd,ld->rl", errors, words[step], preferred_element_type=jnp.float32)
        slopes = (slopes * sigmas[step]).astype(jnp.bfloat16)
        total = jnp.einsum("rl,rd->ld", codes[step], errors, preferred_element_type=jnp.float32)
        return total + jnp.einsum("rl,rd->ld", slopes, rows, preferred_element_type=jnp.float32)

    def send(x):
        return x.astype(jnp.bfloat16)

    far = grads_of(half)
    up = (to_right(send(far[:cut])), None)
    down = (None, to_left(send(far[cut:])))
    for step in range(half - 1, 0, -1):
        ahead, behind = grads_of(step), grads_of(-step)
        parts = []
        for total, came in ((ahead, up), (behind, down)):
            pieces = (total[:cut], total[cut:])
            parts.append(
                [send(p if c is None else p + c.astype(jnp.float32)) for p, c in zip(pieces, came)]
            )
        up = tuple(to_right(p) for p in parts[0])
        down = tuple(to_left(p) for p in parts[1])
    own = grads_of(0)
    halves = []
    for i, part in enumerate((own[:cut], own[cut:])):
        for came in (up[i], down[i]):
            if came is not None:
                part = part + came.astype(jnp.float32)
        halves.append(part)
    return (jnp.concatenate(halves) / block_rows).astype(jnp.bfloat16)


def solution(mesh):
    in_specs = (
        P(("grp", "row"), "lat", None),
        P("grp", None),
        P(("grp", "lat", "row"), None),
        P(("grp", "lat", "row")),
        P("grp"),
    )
    out_specs = P(("grp", "lat", "row"), None)
    lat_count, row_count = mesh.shape["lat"], mesh.shape["row"]

    def body(activations, act_blocks, dictionary, enc_bias, dec_bias):
        gathered = lat_count * dictionary.size * dictionary.dtype.itemsize
        fits = row_count == 2 and lat_count % 2 == 0 and gathered <= GATHER_LIMIT
        step = ring_body if fits else exchange_body
        return step(activations, act_blocks, dictionary, enc_bias, dec_bias)

    return jax.shard_map(body, mesh=mesh, in_specs=in_specs, out_specs=out_specs, check_vma=False)
```

```python
from functools import partial

import jax
import jax.numpy as jnp
from jax import lax
from jax.experimental import pallas as pl
from jax.experimental.pallas import tpu as pltpu
from jax.sharding import PartitionSpec as P

GATHER_LIMIT = 32 * 2**20
LANES = 128


def slot_tables(lists, block_count, slot_count):
    row_total = lists.shape[0]
    labels = jnp.arange(block_count, dtype=jnp.int32)
    matches = jnp.sum((lists[:, :, None] == labels[None, None, :]).astype(jnp.int32), axis=1)
    position = jnp.cumsum(matches, axis=0) - 1
    places = jnp.arange(slot_count, dtype=jnp.int32)
    hits = ((matches[:, :, None] == 1) & (position[:, :, None] == places[None, None, :])).astype(
        jnp.int32
    )
    row_ids = jnp.arange(row_total, dtype=jnp.int32)
    table = jnp.sum(hits * row_ids[:, None, None], axis=0)
    filled = jnp.sum(hits, axis=0)
    return (table, filled)


def encode_slot(dict_full, bias_full, slot_rows, is_filled):
    latent_width = dict_full.shape[0]

    def encode_active(inputs):
        preacts = jnp.einsum("rd,ld->rl", inputs, dict_full, preferred_element_type=jnp.float32)
        preacts = preacts + bias_full.astype(jnp.float32)
        latent_codes = jax.nn.softplus(preacts).astype(jnp.bfloat16)
        pieces = jnp.einsum(
            "rl,ld->rd", latent_codes, dict_full, preferred_element_type=jnp.float32
        )
        return (latent_codes, jax.nn.sigmoid(preacts), pieces.astype(jnp.bfloat16))

    def encode_vacant(inputs):
        return (
            jnp.zeros((inputs.shape[0], latent_width), jnp.bfloat16),
            jnp.zeros((inputs.shape[0], latent_width), jnp.float32),
            jnp.zeros_like(inputs),
        )

    return lax.cond(is_filled > 0, encode_active, encode_vacant, slot_rows)


def slope_slot(dict_full, err_rows, sigmas, is_filled):

    def slope_active(err_in, sig_in):
        code_grads = jnp.einsum("rd,ld->rl", err_in, dict_full, preferred_element_type=jnp.float32)
        return (code_grads * sig_in).astype(jnp.bfloat16)

    def slope_vacant(err_in, sig_in):
        return jnp.zeros(sig_in.shape, jnp.bfloat16)

    return lax.cond(is_filled > 0, slope_active, slope_vacant, err_rows, sigmas)


def exchange_body(activations, act_blocks, dictionary, enc_bias, dec_bias):
    lat_count = lax.axis_size("lat")
    row_count = lax.axis_size("row")
    lat_index = lax.axis_index("lat")
    row_index = lax.axis_index("row")
    half_blocks, rows_each, feature_dim = activations.shape
    list_width = act_blocks.shape[1]
    slot_count = list_width * half_blocks // lat_count
    block_rows = rows_each * lat_count
    flat_width = rows_each * feature_dim
    dict_full, bias_full = (
        lax.all_gather(dictionary, "row", axis=0, tiled=True),
        lax.all_gather(enc_bias, "row", axis=0, tiled=True),
    )
    flat_acts = activations.reshape(half_blocks, flat_width)
    bias_flat = jnp.tile(dec_bias.astype(jnp.float32), rows_each)
    centred = (flat_acts.astype(jnp.float32) - bias_flat[None, :]).astype(jnp.bfloat16)
    lists = act_blocks.reshape(row_count, half_blocks, list_width)
    tables, filled = jax.vmap(partial(slot_tables, block_count=lat_count, slot_count=slot_count))(
        lists
    )
    own_table = lax.dynamic_index_in_dim(tables, row_index, 0, keepdims=False)
    own_filled = lax.dynamic_index_in_dim(filled, row_index, 0, keepdims=False)
    mine_filled = lax.dynamic_index_in_dim(filled, lat_index, 1, keepdims=False)
    send_rows = own_table.T
    send_live = own_filled.T
    slot_flags = lax.dynamic_index_in_dim(mine_filled, row_index, 0, keepdims=False)
    wire_shape = (slot_count, block_rows, feature_dim)
    mask_bf = send_live.astype(jnp.bfloat16)[..., None]
    mask_f = send_live.astype(jnp.float32)[..., None]
    back_shape = send_rows.shape + (flat_width,)
    outgoing = (centred[send_rows] * mask_bf).reshape(wire_shape)
    items = lax.all_to_all(outgoing, "lat", split_axis=1, concat_axis=1, tiled=True)
    latent_codes, sigmas, pieces = lax.map(
        lambda bundle: encode_slot(dict_full, bias_full, bundle[0], bundle[1]), (items, slot_flags)
    )
    returned = lax.all_to_all(pieces, "lat", split_axis=1, concat_axis=1, tiled=True)
    returned = returned.reshape(back_shape).astype(jnp.float32) * mask_f
    rebuilt = jnp.zeros((half_blocks, flat_width), jnp.float32).at[send_rows].add(returned)
    errors = (rebuilt - centred.astype(jnp.float32)).astype(jnp.bfloat16)
    err_out = (errors[send_rows] * mask_bf).reshape(wire_shape)
    err_items = lax.all_to_all(err_out, "lat", split_axis=1, concat_axis=1, tiled=True)
    slopes = lax.map(
        lambda bundle: slope_slot(dict_full, bundle[0], bundle[1], bundle[2]),
        (err_items, sigmas, slot_flags),
    )
    total = jnp.einsum("srl,srd->ld", latent_codes, err_items, preferred_element_type=jnp.float32)
    total = total + jnp.einsum("srl,srd->ld", slopes, items, preferred_element_type=jnp.float32)
    grads = lax.psum_scatter(total / block_rows, "row", scatter_dimension=0, tiled=True)
    return grads.astype(jnp.bfloat16)


def after(values, token):
    anywhere = pl.BlockSpec(memory_space=pl.ANY)

    def nothing(*refs):
        del refs

    return pl.pallas_call(
        nothing,
        out_shape=[jax.ShapeDtypeStruct(v.shape, v.dtype) for v in values],
        in_specs=[anywhere] * (len(values) + 1),
        out_specs=[anywhere] * len(values),
        input_output_aliases={i: i for i in range(len(values))},
        compiler_params=pltpu.CompilerParams(vmem_limit_bytes=2**20),
        cost_estimate=pl.CostEstimate(flops=0, bytes_accessed=0, transcendentals=0),
    )(*values, token)


def ring_body(activations, act_blocks, dictionary, enc_bias, dec_bias):
    count = lax.axis_size("lat")
    lat_index = lax.axis_index("lat")
    row_index = lax.axis_index("row")
    half_blocks, rows_each, width = activations.shape
    latents = dictionary.shape[0]
    cut = latents // 2
    block_rows = rows_each * count
    half = count // 2

    order = list(range(0, count, 2)) + list(range(count - 1, 0, -2))
    right_pairs = [(order[i], order[(i + 1) % count]) for i in range(count)]
    left_pairs = [(b, a) for a, b in right_pairs]
    place = jnp.where(lat_index % 2 == 0, lat_index // 2, count - 1 - lat_index // 2)

    def to_right(x):
        return lax.ppermute(x, "lat", right_pairs)

    def to_left(x):
        return lax.ppermute(x, "lat", left_pairs)

    def to_core(x):
        return lax.ppermute(x, "row", [(0, 1), (1, 0)])

    def owner(step):
        at = (place + step + count) % count
        return jnp.where(at < half, 2 * at, 2 * (count - 1 - at) + 1)

    first = jnp.arange(LANES) == 0
    tail = jnp.where(first, enc_bias[:, None], jnp.zeros((), enc_bias.dtype))
    own_words = jnp.concatenate([dictionary, tail], axis=1)
    words = {0: own_words}
    from_left = from_right = (own_words[:cut], own_words[cut:])
    for step in range(1, half):
        from_left = tuple(to_right(x) for x in from_left)
        from_right = tuple(to_left(x) for x in from_right[::-1])[::-1]
        words[-step], words[step] = jnp.concatenate(from_left), jnp.concatenate(from_right)
    words[half] = jnp.concatenate([to_right(from_left[0]), to_left(from_right[1])])

    centred = (activations.astype(jnp.float32) - dec_bias.astype(jnp.float32)).astype(jnp.bfloat16)
    centred = centred.reshape(half_blocks * rows_each, width)
    rows = jnp.concatenate([centred, to_core(centred)])
    ones = jnp.broadcast_to(first.astype(rows.dtype), (rows.shape[0], LANES))
    rows_one = jnp.concatenate([rows, ones], axis=1)
    lists = act_blocks.reshape(2, half_blocks, act_blocks.shape[1])
    lists = jnp.where(row_index == 0, lists, lists[::-1]).reshape(2 * half_blocks, -1)

    steps = [0] + [s for t in range(1, half) for s in (-t, t)] + [half]
    owners = jnp.stack([owner(s) for s in steps])
    listed = jnp.any(lists[:, :, None] == owners, axis=1).astype(jnp.float32)
    listed = lax.optimization_barrier(jnp.repeat(listed, rows_each, axis=0))

    codes, sigmas = {}, {}
    rebuilt = None
    for i, step in enumerate(steps):
        mask = listed[:, i : i + 1] > 0
        preacts = jnp.einsum("rd,ld->rl", rows_one, words[step], preferred_element_type=jnp.float32)
        code = jnp.where(mask, jax.nn.softplus(preacts), 0.0).astype(jnp.bfloat16)
        sigma = jnp.where(mask, jax.nn.sigmoid(preacts), 0.0)
        codes[step], sigmas[step] = lax.optimization_barrier((code, sigma))
        pieces = jnp.einsum(
            "rl,ld->rd", codes[step], words[step][:, :width], preferred_element_type=jnp.float32
        )
        rebuilt = pieces if rebuilt is None else rebuilt + pieces
    rebuilt = rebuilt.astype(jnp.bfloat16)
    swapped = to_core(rebuilt)
    middle = half_blocks * rows_each
    swapped = jnp.concatenate([swapped[middle:], swapped[:middle]])
    errors = rebuilt.astype(jnp.float32) + swapped.astype(jnp.float32) - rows.astype(jnp.float32)
    errors = errors.astype(jnp.bfloat16)

    def grads_of(step, token):
        code, sigma = codes[step], sigmas[step]
        if token is not None:
            code, sigma = after((code, sigma), token)
        slopes = jnp.einsum(
            "rd,ld->rl", errors, words[step][:, :width], preferred_element_type=jnp.float32
        )
        slopes = lax.optimization_barrier((slopes * sigma).astype(jnp.bfloat16))
        total = jnp.einsum("rl,rd->ld", code, errors, preferred_element_type=jnp.float32)
        return total + jnp.einsum("rl,rd->ld", slopes, rows, preferred_element_type=jnp.float32)

    def send(x):
        return x.astype(jnp.bfloat16)

    far = send(grads_of(half, None))
    up = (to_right(far[:cut]), None)
    down = (None, to_left(far[cut:]))
    tokens = (far, far)
    for step in range(half - 1, 0, -1):
        ahead, behind = grads_of(step, tokens[0]), grads_of(-step, tokens[1])
        tokens = (up[0], down[1])
        parts = []
        for total, came in ((ahead, up), (behind, down)):
            pieces = (total[:cut], total[cut:])
            parts.append(
                [send(p if c is None else p + c.astype(jnp.float32)) for p, c in zip(pieces, came)]
            )
        up = tuple(to_right(p) for p in parts[0])
        down = tuple(to_left(p) for p in parts[1])
    own = grads_of(0, tokens[0])
    halves = []
    for i, part in enumerate((own[:cut], own[cut:])):
        for came in (up[i], down[i]):
            if came is not None:
                part = part + came.astype(jnp.float32)
        halves.append(part)
    return (jnp.concatenate(halves) / block_rows).astype(jnp.bfloat16)


def solution(mesh):
    in_specs = (
        P(("grp", "row"), "lat", None),
        P("grp", None),
        P(("grp", "lat", "row"), None),
        P(("grp", "lat", "row")),
        P("grp"),
    )
    out_specs = P(("grp", "lat", "row"), None)
    lat_count, row_count = mesh.shape["lat"], mesh.shape["row"]

    def body(activations, act_blocks, dictionary, enc_bias, dec_bias):
        gathered = lat_count * dictionary.size * dictionary.dtype.itemsize
        fits = row_count == 2 and lat_count % 2 == 0 and gathered <= GATHER_LIMIT
        step = ring_body if fits else exchange_body
        return step(activations, act_blocks, dictionary, enc_bias, dec_bias)

    return jax.shard_map(body, mesh=mesh, in_specs=in_specs, out_specs=out_specs, check_vma=False)
```

```python
from functools import partial

import jax
import jax.numpy as jnp
from jax import lax
from jax.experimental import pallas as pl
from jax.experimental.pallas import tpu as pltpu
from jax.sharding import PartitionSpec as P

GATHER_LIMIT = 32 * 2**20
TILES = 4


def slot_tables(lists, block_count, slot_count):
    row_total = lists.shape[0]
    labels = jnp.arange(block_count, dtype=jnp.int32)
    matches = jnp.sum((lists[:, :, None] == labels[None, None, :]).astype(jnp.int32), axis=1)
    position = jnp.cumsum(matches, axis=0) - 1
    places = jnp.arange(slot_count, dtype=jnp.int32)
    hits = ((matches[:, :, None] == 1) & (position[:, :, None] == places[None, None, :])).astype(
        jnp.int32
    )
    row_ids = jnp.arange(row_total, dtype=jnp.int32)
    table = jnp.sum(hits * row_ids[:, None, None], axis=0)
    filled = jnp.sum(hits, axis=0)
    return (table, filled)


def encode_slot(dict_full, bias_full, slot_rows, is_filled):
    latent_width = dict_full.shape[0]

    def encode_active(inputs):
        preacts = jnp.einsum("rd,ld->rl", inputs, dict_full, preferred_element_type=jnp.float32)
        preacts = preacts + bias_full.astype(jnp.float32)
        latent_codes = jax.nn.softplus(preacts).astype(jnp.bfloat16)
        pieces = jnp.einsum(
            "rl,ld->rd", latent_codes, dict_full, preferred_element_type=jnp.float32
        )
        return (latent_codes, jax.nn.sigmoid(preacts), pieces.astype(jnp.bfloat16))

    def encode_vacant(inputs):
        return (
            jnp.zeros((inputs.shape[0], latent_width), jnp.bfloat16),
            jnp.zeros((inputs.shape[0], latent_width), jnp.float32),
            jnp.zeros_like(inputs),
        )

    return lax.cond(is_filled > 0, encode_active, encode_vacant, slot_rows)


def slope_slot(dict_full, err_rows, sigmas, is_filled):

    def slope_active(err_in, sig_in):
        code_grads = jnp.einsum("rd,ld->rl", err_in, dict_full, preferred_element_type=jnp.float32)
        return (code_grads * sig_in).astype(jnp.bfloat16)

    def slope_vacant(err_in, sig_in):
        return jnp.zeros(sig_in.shape, jnp.bfloat16)

    return lax.cond(is_filled > 0, slope_active, slope_vacant, err_rows, sigmas)


def exchange_body(activations, act_blocks, dictionary, enc_bias, dec_bias):
    lat_count = lax.axis_size("lat")
    row_count = lax.axis_size("row")
    lat_index = lax.axis_index("lat")
    row_index = lax.axis_index("row")
    half_blocks, rows_each, feature_dim = activations.shape
    list_width = act_blocks.shape[1]
    slot_count = list_width * half_blocks // lat_count
    block_rows = rows_each * lat_count
    flat_width = rows_each * feature_dim
    dict_full, bias_full = (
        lax.all_gather(dictionary, "row", axis=0, tiled=True),
        lax.all_gather(enc_bias, "row", axis=0, tiled=True),
    )
    flat_acts = activations.reshape(half_blocks, flat_width)
    bias_flat = jnp.tile(dec_bias.astype(jnp.float32), rows_each)
    centred = (flat_acts.astype(jnp.float32) - bias_flat[None, :]).astype(jnp.bfloat16)
    lists = act_blocks.reshape(row_count, half_blocks, list_width)
    tables, filled = jax.vmap(partial(slot_tables, block_count=lat_count, slot_count=slot_count))(
        lists
    )
    own_table = lax.dynamic_index_in_dim(tables, row_index, 0, keepdims=False)
    own_filled = lax.dynamic_index_in_dim(filled, row_index, 0, keepdims=False)
    mine_filled = lax.dynamic_index_in_dim(filled, lat_index, 1, keepdims=False)
    send_rows = own_table.T
    send_live = own_filled.T
    slot_flags = lax.dynamic_index_in_dim(mine_filled, row_index, 0, keepdims=False)
    wire_shape = (slot_count, block_rows, feature_dim)
    mask_bf = send_live.astype(jnp.bfloat16)[..., None]
    mask_f = send_live.astype(jnp.float32)[..., None]
    back_shape = send_rows.shape + (flat_width,)
    outgoing = (centred[send_rows] * mask_bf).reshape(wire_shape)
    items = lax.all_to_all(outgoing, "lat", split_axis=1, concat_axis=1, tiled=True)
    latent_codes, sigmas, pieces = lax.map(
        lambda bundle: encode_slot(dict_full, bias_full, bundle[0], bundle[1]), (items, slot_flags)
    )
    returned = lax.all_to_all(pieces, "lat", split_axis=1, concat_axis=1, tiled=True)
    returned = returned.reshape(back_shape).astype(jnp.float32) * mask_f
    rebuilt = jnp.zeros((half_blocks, flat_width), jnp.float32).at[send_rows].add(returned)
    errors = (rebuilt - centred.astype(jnp.float32)).astype(jnp.bfloat16)
    err_out = (errors[send_rows] * mask_bf).reshape(wire_shape)
    err_items = lax.all_to_all(err_out, "lat", split_axis=1, concat_axis=1, tiled=True)
    slopes = lax.map(
        lambda bundle: slope_slot(dict_full, bundle[0], bundle[1], bundle[2]),
        (err_items, sigmas, slot_flags),
    )
    total = jnp.einsum("srl,srd->ld", latent_codes, err_items, preferred_element_type=jnp.float32)
    total = total + jnp.einsum("srl,srd->ld", slopes, items, preferred_element_type=jnp.float32)
    grads = lax.psum_scatter(total / block_rows, "row", scatter_dimension=0, tiled=True)
    return grads.astype(jnp.bfloat16)


def after(values, *tokens):
    anywhere = pl.BlockSpec(memory_space=pl.ANY)

    def nothing(*refs):
        del refs

    return pl.pallas_call(
        nothing,
        out_shape=[jax.ShapeDtypeStruct(v.shape, v.dtype) for v in values],
        in_specs=[anywhere] * (len(values) + len(tokens)),
        out_specs=[anywhere] * len(values),
        input_output_aliases={i: i for i in range(len(values))},
        compiler_params=pltpu.CompilerParams(vmem_limit_bytes=2**20),
        cost_estimate=pl.CostEstimate(flops=0, bytes_accessed=0, transcendentals=0),
    )(*values, *tokens)


def local_call(
    kernel, grid, in_specs, out_specs, out_shape, args, aliases=None, scratch=(), cost=(0, 0)
):
    return pl.pallas_call(
        kernel,
        grid=grid,
        in_specs=in_specs,
        out_specs=out_specs,
        out_shape=out_shape,
        scratch_shapes=scratch,
        input_output_aliases=aliases or {},
        compiler_params=pltpu.CompilerParams(vmem_limit_bytes=24 * 2**20),
        cost_estimate=pl.CostEstimate(flops=cost[0], bytes_accessed=cost[1], transcendentals=0),
    )(*args)


def whole(x):
    return pl.BlockSpec(x.shape, lambda i: (0,) * x.ndim)


def columns(x, tile):
    return pl.BlockSpec((x.shape[0], tile), lambda i: (0, i))


def centre(mine, theirs, dec_bias):
    count, width = mine.shape

    def kernel(x_ref, y_ref, b_ref, o_ref):
        shift = b_ref[...].astype(jnp.float32)
        o_ref[:count, :] = (x_ref[...].astype(jnp.float32) - shift).astype(o_ref.dtype)
        o_ref[count:, :] = (y_ref[...].astype(jnp.float32) - shift).astype(o_ref.dtype)

    tile = width // TILES
    out = jax.ShapeDtypeStruct((2 * count, width), jnp.bfloat16)
    args = (mine, theirs, dec_bias)
    return local_call(kernel, (TILES,), [columns(x, tile) for x in args], columns(out, tile), out, args)


def product(x, y, dims):
    return lax.dot_general(x, y, (dims, ((), ())), preferred_element_type=jnp.float32)


def encode(rows, words, bias, listed, which):
    count, tile = words.shape[0], rows.shape[1] // TILES

    def kernel(x_ref, w_ref, b_ref, m_ref, c_ref, s_ref, acc):
        @pl.when(pl.program_id(0) == 0)
        def _():
            acc[...] = jnp.broadcast_to(b_ref[which : which + 1, :], acc.shape)

        acc[...] += product(x_ref[...], w_ref[...], ((1,), (1,)))

        @pl.when(pl.program_id(0) == TILES - 1)
        def _():
            p = acc[...]
            mask = m_ref[:, which : which + 1] > 0
            code = jnp.maximum(p, 0.0) + jnp.log1p(jnp.exp(-jnp.abs(p)))
            c_ref[...] = jnp.where(mask, code, 0.0).astype(c_ref.dtype)
            s_ref[...] = jnp.where(mask, jax.nn.sigmoid(p), 0.0)

    shape = (rows.shape[0], count)
    out = [jax.ShapeDtypeStruct(shape, jnp.bfloat16), jax.ShapeDtypeStruct(shape, jnp.float32)]
    return local_call(
        kernel,
        (TILES,),
        [columns(rows, tile), columns(words, tile), whole(bias), whole(listed)],
        [whole(o) for o in out],
        out,
        (rows, words, bias, listed),
        scratch=[pltpu.VMEM(shape, jnp.float32)],
    )


def decode(codes, words, total):
    tile = words.shape[1] // TILES

    def kernel(c_ref, w_ref, *rest):
        part = product(c_ref[...], w_ref[...], ((1,), (0,)))
        rest[-1][...] = part if len(rest) == 1 else part + rest[0][...]

    out = jax.ShapeDtypeStruct((codes.shape[0], words.shape[1]), jnp.float32)
    args = (codes, words) if total is None else (codes, words, total)
    specs = [whole(codes), columns(words, tile)] + [columns(out, tile)] * (len(args) - 2)
    aliases = {2: 0} if len(args) == 3 else None
    return local_call(kernel, (TILES,), specs, columns(out, tile), out, args, aliases)


def slope(errors, words, sigma):
    tile = words.shape[1] // TILES

    def kernel(e_ref, w_ref, s_ref, o_ref, acc):
        @pl.when(pl.program_id(0) == 0)
        def _():
            acc[...] = jnp.zeros_like(acc)

        acc[...] += product(e_ref[...], w_ref[...], ((1,), (1,)))

        @pl.when(pl.program_id(0) == TILES - 1)
        def _():
            o_ref[...] = (acc[...] * s_ref[...]).astype(o_ref.dtype)

    return local_call(
        kernel,
        (TILES,),
        [columns(errors, tile), columns(words, tile), whole(sigma)],
        whole(sigma),
        jax.ShapeDtypeStruct(sigma.shape, jnp.bfloat16),
        (errors, words, sigma),
        scratch=[pltpu.VMEM(sigma.shape, jnp.float32)],
        cost=(2 * sigma.size * words.shape[1], 2 * (errors.size + words.size)),
    )


def gradient(codes, slopes, errors, rows):
    tile = rows.shape[1] // TILES

    def kernel(c_ref, s_ref, e_ref, x_ref, o_ref):
        part = product(c_ref[...], e_ref[...], ((0,), (0,)))
        o_ref[...] = part + product(s_ref[...], x_ref[...], ((0,), (0,)))

    out = jax.ShapeDtypeStruct((codes.shape[1], rows.shape[1]), jnp.float32)
    return local_call(
        kernel,
        (TILES,),
        [whole(codes), whole(slopes), columns(errors, tile), columns(rows, tile)],
        columns(out, tile),
        out,
        (codes, slopes, errors, rows),
        cost=(4 * codes.size * rows.shape[1], 4 * (rows.size + out.size)),
    )


def ring_body(activations, act_blocks, dictionary, enc_bias, dec_bias):
    count = lax.axis_size("lat")
    lat_index = lax.axis_index("lat")
    row_index = lax.axis_index("row")
    half_blocks, rows_each, width = activations.shape
    latents = dictionary.shape[0]
    cut = latents // 2
    block_rows = rows_each * count
    half = count // 2

    order = list(range(0, count, 2)) + list(range(count - 1, 0, -2))
    right_pairs = [(order[i], order[(i + 1) % count]) for i in range(count)]
    left_pairs = [(b, a) for a, b in right_pairs]
    place = jnp.where(lat_index % 2 == 0, lat_index // 2, count - 1 - lat_index // 2)

    def to_right(x):
        return lax.ppermute(x, "lat", right_pairs)

    def to_left(x):
        return lax.ppermute(x, "lat", left_pairs)

    def to_core(x):
        return lax.ppermute(x, "row", [(0, 1), (1, 0)])

    def owner(step):
        at = (place + step + count) % count
        return jnp.where(at < half, 2 * at, 2 * (count - 1 - at) + 1)

    lists = act_blocks.reshape(2, half_blocks, act_blocks.shape[1])
    lists = jnp.where(row_index == 0, lists, lists[::-1]).reshape(2 * half_blocks, -1)
    steps = [0] + [s for t in range(1, half) for s in (-t, t)] + [half]
    owners = jnp.stack([owner(s) for s in steps])
    listed = jnp.any(lists[:, :, None] == owners, axis=1).astype(jnp.float32)
    listed = jnp.repeat(listed, rows_each, axis=0)

    biases = jnp.broadcast_to(enc_bias.reshape(1, latents), (count, latents))
    biases = lax.all_to_all(biases, "lat", split_axis=0, concat_axis=0, tiled=True)
    pick = (owners[:, None] == jnp.arange(count)).astype(biases.dtype)
    biases = jnp.einsum("so,ol->sl", pick, biases, preferred_element_type=jnp.float32)

    acts = activations.reshape(half_blocks * rows_each, width)
    rows = None

    words = {0: dictionary}
    codes, sigmas, rebuilt = {}, {}, None
    for t in range(1, half):
        arrived = to_right(words[1 - t]), to_left(words[t - 1])
        if t == 1:
            words[-1], words[1] = after(arrived, biases)
            (shift,) = after((dec_bias.reshape(1, width),), words[1])
            rows = centre(acts, to_core(acts), shift)
        else:
            words[-t], words[t] = after(arrived, rebuilt)
        for step in (-t, t) if t > 1 else (0, -t, t):
            which = steps.index(step)
            codes[step], sigmas[step] = encode(rows, words[step], biases, listed, which)
            rebuilt = decode(codes[step], words[step], rebuilt)
    last = to_right(words[1 - half][:cut]), to_left(words[half - 1][cut:])
    words[half] = jnp.concatenate(after(last, rebuilt))
    preacts = jnp.einsum("rd,ld->rl", rows, words[half], preferred_element_type=jnp.float32)
    preacts = preacts + biases[-1:]
    mask = listed[:, len(steps) - 1 :] > 0
    code = jnp.where(mask, jax.nn.softplus(preacts), 0.0).astype(jnp.bfloat16)
    sigma = jnp.where(mask, jax.nn.sigmoid(preacts), 0.0)
    codes[half], sigmas[half] = lax.optimization_barrier((code, sigma))
    rebuilt = rebuilt + jnp.einsum(
        "rl,ld->rd", codes[half], words[half], preferred_element_type=jnp.float32
    )
    rebuilt = rebuilt.astype(jnp.bfloat16)
    swapped = to_core(rebuilt)
    middle = half_blocks * rows_each
    swapped = jnp.concatenate([swapped[middle:], swapped[:middle]])
    errors = rebuilt.astype(jnp.float32) + swapped.astype(jnp.float32) - rows.astype(jnp.float32)
    errors = errors.astype(jnp.bfloat16)

    def grads_of(step, token):
        (sigma,) = after((sigmas[step],), token)
        slopes = slope(errors, words[step], sigma)
        return gradient(codes[step], slopes, errors, rows)

    def send(x):
        return x.astype(jnp.bfloat16)

    slopes = jnp.einsum("rd,ld->rl", errors, words[half], preferred_element_type=jnp.float32)
    slopes = lax.optimization_barrier((slopes * sigmas[half]).astype(jnp.bfloat16))
    far = jnp.einsum("rl,rd->ld", codes[half], errors, preferred_element_type=jnp.float32)
    far = send(far + jnp.einsum("rl,rd->ld", slopes, rows, preferred_element_type=jnp.float32))
    up = (to_right(far[:cut]), None)
    down = (None, to_left(far[cut:]))
    tokens = (far, far)
    for step in range(half - 1, 0, -1):
        ahead, behind = grads_of(step, tokens[0]), grads_of(-step, tokens[1])
        tokens = (up[0], down[1])
        parts = []
        for total, came in ((ahead, up), (behind, down)):
            pieces = (total[:cut], total[cut:])
            parts.append(
                [send(p if c is None else p + c.astype(jnp.float32)) for p, c in zip(pieces, came)]
            )
        up = tuple(to_right(p) for p in parts[0])
        down = tuple(to_left(p) for p in parts[1])
    own = grads_of(0, tokens[0])
    halves = []
    for i, part in enumerate((own[:cut], own[cut:])):
        for came in (up[i], down[i]):
            if came is not None:
                part = part + came.astype(jnp.float32)
        halves.append(part)
    return (jnp.concatenate(halves) / block_rows).astype(jnp.bfloat16)


def solution(mesh):
    in_specs = (
        P(("grp", "row"), "lat", None),
        P("grp", None),
        P(("grp", "lat", "row"), None),
        P(("grp", "lat", "row")),
        P("grp"),
    )
    out_specs = P(("grp", "lat", "row"), None)
    lat_count, row_count = mesh.shape["lat"], mesh.shape["row"]

    def body(activations, act_blocks, dictionary, enc_bias, dec_bias):
        gathered = lat_count * dictionary.size * dictionary.dtype.itemsize
        fits = row_count == 2 and lat_count % 2 == 0 and gathered <= GATHER_LIMIT
        step = ring_body if fits else exchange_body
        return step(activations, act_blocks, dictionary, enc_bias, dec_bias)

    return jax.shard_map(body, mesh=mesh, in_specs=in_specs, out_specs=out_specs, check_vma=False)
```

```python
from functools import partial

import jax
import jax.numpy as jnp
from jax import lax
from jax.experimental import pallas as pl
from jax.experimental.pallas import tpu as pltpu
from jax.sharding import PartitionSpec as P

GATHER_LIMIT = 32 * 2**20
TILES = 4


def slot_tables(lists, block_count, slot_count):
    row_total = lists.shape[0]
    labels = jnp.arange(block_count, dtype=jnp.int32)
    matches = jnp.sum((lists[:, :, None] == labels[None, None, :]).astype(jnp.int32), axis=1)
    position = jnp.cumsum(matches, axis=0) - 1
    places = jnp.arange(slot_count, dtype=jnp.int32)
    hits = ((matches[:, :, None] == 1) & (position[:, :, None] == places[None, None, :])).astype(
        jnp.int32
    )
    row_ids = jnp.arange(row_total, dtype=jnp.int32)
    table = jnp.sum(hits * row_ids[:, None, None], axis=0)
    filled = jnp.sum(hits, axis=0)
    return (table, filled)


def encode_slot(dict_full, bias_full, slot_rows, is_filled):
    latent_width = dict_full.shape[0]

    def encode_active(inputs):
        preacts = jnp.einsum("rd,ld->rl", inputs, dict_full, preferred_element_type=jnp.float32)
        preacts = preacts + bias_full.astype(jnp.float32)
        latent_codes = jax.nn.softplus(preacts).astype(jnp.bfloat16)
        pieces = jnp.einsum(
            "rl,ld->rd", latent_codes, dict_full, preferred_element_type=jnp.float32
        )
        return (latent_codes, jax.nn.sigmoid(preacts), pieces.astype(jnp.bfloat16))

    def encode_vacant(inputs):
        return (
            jnp.zeros((inputs.shape[0], latent_width), jnp.bfloat16),
            jnp.zeros((inputs.shape[0], latent_width), jnp.float32),
            jnp.zeros_like(inputs),
        )

    return lax.cond(is_filled > 0, encode_active, encode_vacant, slot_rows)


def slope_slot(dict_full, err_rows, sigmas, is_filled):

    def slope_active(err_in, sig_in):
        code_grads = jnp.einsum("rd,ld->rl", err_in, dict_full, preferred_element_type=jnp.float32)
        return (code_grads * sig_in).astype(jnp.bfloat16)

    def slope_vacant(err_in, sig_in):
        return jnp.zeros(sig_in.shape, jnp.bfloat16)

    return lax.cond(is_filled > 0, slope_active, slope_vacant, err_rows, sigmas)


def exchange_body(activations, act_blocks, dictionary, enc_bias, dec_bias):
    lat_count = lax.axis_size("lat")
    row_count = lax.axis_size("row")
    lat_index = lax.axis_index("lat")
    row_index = lax.axis_index("row")
    half_blocks, rows_each, feature_dim = activations.shape
    list_width = act_blocks.shape[1]
    slot_count = list_width * half_blocks // lat_count
    block_rows = rows_each * lat_count
    flat_width = rows_each * feature_dim
    dict_full, bias_full = (
        lax.all_gather(dictionary, "row", axis=0, tiled=True),
        lax.all_gather(enc_bias, "row", axis=0, tiled=True),
    )
    flat_acts = activations.reshape(half_blocks, flat_width)
    bias_flat = jnp.tile(dec_bias.astype(jnp.float32), rows_each)
    centred = (flat_acts.astype(jnp.float32) - bias_flat[None, :]).astype(jnp.bfloat16)
    lists = act_blocks.reshape(row_count, half_blocks, list_width)
    tables, filled = jax.vmap(partial(slot_tables, block_count=lat_count, slot_count=slot_count))(
        lists
    )
    own_table = lax.dynamic_index_in_dim(tables, row_index, 0, keepdims=False)
    own_filled = lax.dynamic_index_in_dim(filled, row_index, 0, keepdims=False)
    mine_filled = lax.dynamic_index_in_dim(filled, lat_index, 1, keepdims=False)
    send_rows = own_table.T
    send_live = own_filled.T
    slot_flags = lax.dynamic_index_in_dim(mine_filled, row_index, 0, keepdims=False)
    wire_shape = (slot_count, block_rows, feature_dim)
    mask_bf = send_live.astype(jnp.bfloat16)[..., None]
    mask_f = send_live.astype(jnp.float32)[..., None]
    back_shape = send_rows.shape + (flat_width,)
    outgoing = (centred[send_rows] * mask_bf).reshape(wire_shape)
    items = lax.all_to_all(outgoing, "lat", split_axis=1, concat_axis=1, tiled=True)
    latent_codes, sigmas, pieces = lax.map(
        lambda bundle: encode_slot(dict_full, bias_full, bundle[0], bundle[1]), (items, slot_flags)
    )
    returned = lax.all_to_all(pieces, "lat", split_axis=1, concat_axis=1, tiled=True)
    returned = returned.reshape(back_shape).astype(jnp.float32) * mask_f
    rebuilt = jnp.zeros((half_blocks, flat_width), jnp.float32).at[send_rows].add(returned)
    errors = (rebuilt - centred.astype(jnp.float32)).astype(jnp.bfloat16)
    err_out = (errors[send_rows] * mask_bf).reshape(wire_shape)
    err_items = lax.all_to_all(err_out, "lat", split_axis=1, concat_axis=1, tiled=True)
    slopes = lax.map(
        lambda bundle: slope_slot(dict_full, bundle[0], bundle[1], bundle[2]),
        (err_items, sigmas, slot_flags),
    )
    total = jnp.einsum("srl,srd->ld", latent_codes, err_items, preferred_element_type=jnp.float32)
    total = total + jnp.einsum("srl,srd->ld", slopes, items, preferred_element_type=jnp.float32)
    grads = lax.psum_scatter(total / block_rows, "row", scatter_dimension=0, tiled=True)
    return grads.astype(jnp.bfloat16)


def after(values, *tokens):
    anywhere = pl.BlockSpec(memory_space=pl.ANY)

    def nothing(*refs):
        del refs

    return pl.pallas_call(
        nothing,
        out_shape=[jax.ShapeDtypeStruct(v.shape, v.dtype) for v in values],
        in_specs=[anywhere] * (len(values) + len(tokens)),
        out_specs=[anywhere] * len(values),
        input_output_aliases={i: i for i in range(len(values))},
        compiler_params=pltpu.CompilerParams(vmem_limit_bytes=2**20),
        cost_estimate=pl.CostEstimate(flops=0, bytes_accessed=0, transcendentals=0),
    )(*values, *tokens)


def local_call(
    kernel, grid, in_specs, out_specs, out_shape, args, aliases=None, scratch=(), cost=(0, 0)
):
    return pl.pallas_call(
        kernel,
        grid=grid,
        in_specs=in_specs,
        out_specs=out_specs,
        out_shape=out_shape,
        scratch_shapes=scratch,
        input_output_aliases=aliases or {},
        compiler_params=pltpu.CompilerParams(vmem_limit_bytes=24 * 2**20),
        cost_estimate=pl.CostEstimate(flops=cost[0], bytes_accessed=cost[1], transcendentals=0),
    )(*args)


def whole(x):
    return pl.BlockSpec(x.shape, lambda i: (0,) * x.ndim)


def columns(x, tile):
    return pl.BlockSpec((x.shape[0], tile), lambda i: (0, i))


def centre(mine, theirs, dec_bias):
    count, width = mine.shape

    def kernel(x_ref, y_ref, b_ref, o_ref):
        shift = b_ref[...].astype(jnp.float32)
        o_ref[:count, :] = (x_ref[...].astype(jnp.float32) - shift).astype(o_ref.dtype)
        o_ref[count:, :] = (y_ref[...].astype(jnp.float32) - shift).astype(o_ref.dtype)

    tile = width // TILES
    out = jax.ShapeDtypeStruct((2 * count, width), jnp.bfloat16)
    args = (mine, theirs, dec_bias)
    return local_call(kernel, (TILES,), [columns(x, tile) for x in args], columns(out, tile), out, args)


def product(x, y, dims):
    return lax.dot_general(x, y, (dims, ((), ())), preferred_element_type=jnp.float32)


def encode(rows, words, bias, listed, which):
    count, tile = words.shape[0], rows.shape[1] // TILES

    def kernel(x_ref, w_ref, b_ref, m_ref, c_ref, s_ref, acc):
        @pl.when(pl.program_id(0) == 0)
        def _():
            acc[...] = jnp.broadcast_to(b_ref[which : which + 1, :], acc.shape)

        acc[...] += product(x_ref[...], w_ref[...], ((1,), (1,)))

        @pl.when(pl.program_id(0) == TILES - 1)
        def _():
            p = acc[...]
            mask = m_ref[:, which : which + 1] > 0
            code = jnp.maximum(p, 0.0) + jnp.log1p(jnp.exp(-jnp.abs(p)))
            c_ref[...] = jnp.where(mask, code, 0.0).astype(c_ref.dtype)
            s_ref[...] = jnp.where(mask, jax.nn.sigmoid(p), 0.0)

    shape = (rows.shape[0], count)
    out = [jax.ShapeDtypeStruct(shape, jnp.bfloat16), jax.ShapeDtypeStruct(shape, jnp.float32)]
    return local_call(
        kernel,
        (TILES,),
        [columns(rows, tile), columns(words, tile), whole(bias), whole(listed)],
        [whole(o) for o in out],
        out,
        (rows, words, bias, listed),
        scratch=[pltpu.VMEM(shape, jnp.float32)],
    )


def decode(codes, words, total):
    tile = words.shape[1] // TILES

    def kernel(c_ref, w_ref, *rest):
        part = product(c_ref[...], w_ref[...], ((1,), (0,)))
        rest[-1][...] = part if len(rest) == 1 else part + rest[0][...]

    out = jax.ShapeDtypeStruct((codes.shape[0], words.shape[1]), jnp.float32)
    args = (codes, words) if total is None else (codes, words, total)
    specs = [whole(codes), columns(words, tile)] + [columns(out, tile)] * (len(args) - 2)
    aliases = {2: 0} if len(args) == 3 else None
    return local_call(kernel, (TILES,), specs, columns(out, tile), out, args, aliases)


def slope(errors, words, sigma):
    tile = words.shape[1] // TILES

    def kernel(e_ref, w_ref, s_ref, o_ref, acc):
        @pl.when(pl.program_id(0) == 0)
        def _():
            acc[...] = jnp.zeros_like(acc)

        acc[...] += product(e_ref[...], w_ref[...], ((1,), (1,)))

        @pl.when(pl.program_id(0) == TILES - 1)
        def _():
            o_ref[...] = (acc[...] * s_ref[...]).astype(o_ref.dtype)

    return local_call(
        kernel,
        (TILES,),
        [columns(errors, tile), columns(words, tile), whole(sigma)],
        whole(sigma),
        jax.ShapeDtypeStruct(sigma.shape, jnp.bfloat16),
        (errors, words, sigma),
        scratch=[pltpu.VMEM(sigma.shape, jnp.float32)],
        cost=(2 * sigma.size * words.shape[1], 2 * (errors.size + words.size)),
    )


def gradient(codes, slopes, errors, rows):
    tile = rows.shape[1] // TILES

    def kernel(c_ref, s_ref, e_ref, x_ref, o_ref):
        part = product(c_ref[...], e_ref[...], ((0,), (0,)))
        o_ref[...] = part + product(s_ref[...], x_ref[...], ((0,), (0,)))

    out = jax.ShapeDtypeStruct((codes.shape[1], rows.shape[1]), jnp.float32)
    return local_call(
        kernel,
        (TILES,),
        [whole(codes), whole(slopes), columns(errors, tile), columns(rows, tile)],
        columns(out, tile),
        out,
        (codes, slopes, errors, rows),
        cost=(4 * codes.size * rows.shape[1], 4 * (rows.size + out.size)),
    )


def join(total, came, which):
    count, width = total.shape[0] // 2, total.shape[1]
    tile = width // TILES

    def kernel(*refs):
        value = refs[0][...]
        for ref in refs[1:-1]:
            value = value + ref[...].astype(jnp.float32)
        refs[-1][...] = value.astype(refs[-1].dtype)

    out = jax.ShapeDtypeStruct((count, width), jnp.bfloat16)
    args = (total,) if came is None else (total, came)
    specs = [pl.BlockSpec((count, tile), lambda i: (which, i))]
    specs += [columns(out, tile)] * (len(args) - 1)
    cost = (out.size, 8 * out.size)
    return local_call(kernel, (TILES,), specs, columns(out, tile), out, args, cost=cost)


def finish(total, ups, downs, scale):
    width, cut = total.shape[1], total.shape[0] // 2
    tile = width // TILES

    def kernel(t_ref, *refs):
        for k in range(2):
            half = slice(k * cut, (k + 1) * cut)
            came = refs[k][...].astype(jnp.float32) + refs[2 + k][...].astype(jnp.float32)
            refs[-1][half, :] = ((t_ref[half, :] + came) / scale).astype(refs[-1].dtype)

    out = jax.ShapeDtypeStruct(total.shape, jnp.bfloat16)
    args = (total, *ups, *downs)
    specs = [columns(x, tile) for x in args]
    return local_call(kernel, (TILES,), specs, columns(out, tile), out, args)


def ring_body(activations, act_blocks, dictionary, enc_bias, dec_bias):
    count = lax.axis_size("lat")
    lat_index = lax.axis_index("lat")
    row_index = lax.axis_index("row")
    half_blocks, rows_each, width = activations.shape
    latents = dictionary.shape[0]
    cut = latents // 2
    block_rows = rows_each * count
    half = count // 2

    order = list(range(0, count, 2)) + list(range(count - 1, 0, -2))
    right_pairs = [(order[i], order[(i + 1) % count]) for i in range(count)]
    left_pairs = [(b, a) for a, b in right_pairs]
    place = jnp.where(lat_index % 2 == 0, lat_index // 2, count - 1 - lat_index // 2)

    def to_right(x):
        return lax.ppermute(x, "lat", right_pairs)

    def to_left(x):
        return lax.ppermute(x, "lat", left_pairs)

    def to_core(x):
        return lax.ppermute(x, "row", [(0, 1), (1, 0)])

    def owner(step):
        at = (place + step + count) % count
        return jnp.where(at < half, 2 * at, 2 * (count - 1 - at) + 1)

    lists = act_blocks.reshape(2, half_blocks, act_blocks.shape[1])
    lists = jnp.where(row_index == 0, lists, lists[::-1]).reshape(2 * half_blocks, -1)
    steps = [0] + [s for t in range(1, half) for s in (-t, t)] + [half]
    owners = jnp.stack([owner(s) for s in steps])
    listed = jnp.any(lists[:, :, None] == owners, axis=1).astype(jnp.float32)
    listed = jnp.repeat(listed, rows_each, axis=0)

    biases = jnp.broadcast_to(enc_bias.reshape(1, latents), (count, latents))
    biases = lax.all_to_all(biases, "lat", split_axis=0, concat_axis=0, tiled=True)
    pick = (owners[:, None] == jnp.arange(count)).astype(biases.dtype)
    biases = jnp.einsum("so,ol->sl", pick, biases, preferred_element_type=jnp.float32)

    acts = activations.reshape(half_blocks * rows_each, width)
    rows = None

    words = {0: dictionary}
    codes, sigmas, rebuilt = {}, {}, None
    for t in range(1, half):
        arrived = to_right(words[1 - t]), to_left(words[t - 1])
        if t == 1:
            words[-1], words[1] = after(arrived, biases)
            (shift,) = after((dec_bias.reshape(1, width),), words[1])
            rows = centre(acts, to_core(acts), shift)
        else:
            words[-t], words[t] = after(arrived, rebuilt)
        for step in (-t, t) if t > 1 else (0, -t, t):
            which = steps.index(step)
            codes[step], sigmas[step] = encode(rows, words[step], biases, listed, which)
            rebuilt = decode(codes[step], words[step], rebuilt)
    last = to_right(words[1 - half][:cut]), to_left(words[half - 1][cut:])
    words[half] = jnp.concatenate(after(last, rebuilt))
    preacts = jnp.einsum("rd,ld->rl", rows, words[half], preferred_element_type=jnp.float32)
    preacts = preacts + biases[-1:]
    mask = listed[:, len(steps) - 1 :] > 0
    code = jnp.where(mask, jax.nn.softplus(preacts), 0.0).astype(jnp.bfloat16)
    sigma = jnp.where(mask, jax.nn.sigmoid(preacts), 0.0)
    codes[half], sigmas[half] = lax.optimization_barrier((code, sigma))
    rebuilt = rebuilt + jnp.einsum(
        "rl,ld->rd", codes[half], words[half], preferred_element_type=jnp.float32
    )
    rebuilt = rebuilt.astype(jnp.bfloat16)
    swapped = to_core(rebuilt)
    middle = half_blocks * rows_each
    swapped = jnp.concatenate([swapped[middle:], swapped[:middle]])
    errors = rebuilt.astype(jnp.float32) + swapped.astype(jnp.float32) - rows.astype(jnp.float32)
    errors = errors.astype(jnp.bfloat16)

    def grads_of(step, token):
        (sigma,) = after((sigmas[step],), token)
        slopes = slope(errors, words[step], sigma)
        return gradient(codes[step], slopes, errors, rows)

    def send(x):
        return x.astype(jnp.bfloat16)

    slopes = jnp.einsum("rd,ld->rl", errors, words[half], preferred_element_type=jnp.float32)
    slopes = lax.optimization_barrier((slopes * sigmas[half]).astype(jnp.bfloat16))
    far = jnp.einsum("rl,rd->ld", codes[half], errors, preferred_element_type=jnp.float32)
    far = send(far + jnp.einsum("rl,rd->ld", slopes, rows, preferred_element_type=jnp.float32))
    up = (to_right(far[:cut]), None)
    down = (None, to_left(far[cut:]))
    tokens = (far, far)
    for step in range(half - 1, 0, -1):
        ahead, behind = grads_of(step, tokens[0]), grads_of(-step, tokens[1])
        tokens = (up[0], down[1])
        up = tuple(to_right(join(ahead, came, k)) for k, came in enumerate(up))
        down = tuple(to_left(join(behind, came, k)) for k, came in enumerate(down))
    return finish(grads_of(0, tokens[0]), up, down, block_rows)


def solution(mesh):
    in_specs = (
        P(("grp", "row"), "lat", None),
        P("grp", None),
        P(("grp", "lat", "row"), None),
        P(("grp", "lat", "row")),
        P("grp"),
    )
    out_specs = P(("grp", "lat", "row"), None)
    lat_count, row_count = mesh.shape["lat"], mesh.shape["row"]

    def body(activations, act_blocks, dictionary, enc_bias, dec_bias):
        gathered = lat_count * dictionary.size * dictionary.dtype.itemsize
        fits = row_count == 2 and lat_count % 2 == 0 and gathered <= GATHER_LIMIT
        step = ring_body if fits else exchange_body
        return step(activations, act_blocks, dictionary, enc_bias, dec_bias)

    return jax.shard_map(body, mesh=mesh, in_specs=in_specs, out_specs=out_specs, check_vma=False)
```

```python
from functools import partial

import jax
import jax.numpy as jnp
from jax import lax
from jax.experimental import pallas as pl
from jax.experimental.pallas import tpu as pltpu
from jax.sharding import PartitionSpec as P

GATHER_LIMIT = 32 * 2**20
TILES = 4


def slot_tables(lists, block_count, slot_count):
    row_total = lists.shape[0]
    labels = jnp.arange(block_count, dtype=jnp.int32)
    matches = jnp.sum((lists[:, :, None] == labels[None, None, :]).astype(jnp.int32), axis=1)
    position = jnp.cumsum(matches, axis=0) - 1
    places = jnp.arange(slot_count, dtype=jnp.int32)
    hits = ((matches[:, :, None] == 1) & (position[:, :, None] == places[None, None, :])).astype(
        jnp.int32
    )
    row_ids = jnp.arange(row_total, dtype=jnp.int32)
    table = jnp.sum(hits * row_ids[:, None, None], axis=0)
    filled = jnp.sum(hits, axis=0)
    return (table, filled)


def encode_slot(dict_full, bias_full, slot_rows, is_filled):
    latent_width = dict_full.shape[0]

    def encode_active(inputs):
        preacts = jnp.einsum("rd,ld->rl", inputs, dict_full, preferred_element_type=jnp.float32)
        preacts = preacts + bias_full.astype(jnp.float32)
        latent_codes = jax.nn.softplus(preacts).astype(jnp.bfloat16)
        pieces = jnp.einsum(
            "rl,ld->rd", latent_codes, dict_full, preferred_element_type=jnp.float32
        )
        return (latent_codes, jax.nn.sigmoid(preacts), pieces.astype(jnp.bfloat16))

    def encode_vacant(inputs):
        return (
            jnp.zeros((inputs.shape[0], latent_width), jnp.bfloat16),
            jnp.zeros((inputs.shape[0], latent_width), jnp.float32),
            jnp.zeros_like(inputs),
        )

    return lax.cond(is_filled > 0, encode_active, encode_vacant, slot_rows)


def slope_slot(dict_full, err_rows, sigmas, is_filled):

    def slope_active(err_in, sig_in):
        code_grads = jnp.einsum("rd,ld->rl", err_in, dict_full, preferred_element_type=jnp.float32)
        return (code_grads * sig_in).astype(jnp.bfloat16)

    def slope_vacant(err_in, sig_in):
        return jnp.zeros(sig_in.shape, jnp.bfloat16)

    return lax.cond(is_filled > 0, slope_active, slope_vacant, err_rows, sigmas)


def exchange_body(activations, act_blocks, dictionary, enc_bias, dec_bias):
    lat_count = lax.axis_size("lat")
    row_count = lax.axis_size("row")
    lat_index = lax.axis_index("lat")
    row_index = lax.axis_index("row")
    half_blocks, rows_each, feature_dim = activations.shape
    list_width = act_blocks.shape[1]
    slot_count = list_width * half_blocks // lat_count
    block_rows = rows_each * lat_count
    flat_width = rows_each * feature_dim
    dict_full, bias_full = (
        lax.all_gather(dictionary, "row", axis=0, tiled=True),
        lax.all_gather(enc_bias, "row", axis=0, tiled=True),
    )
    flat_acts = activations.reshape(half_blocks, flat_width)
    bias_flat = jnp.tile(dec_bias.astype(jnp.float32), rows_each)
    centred = (flat_acts.astype(jnp.float32) - bias_flat[None, :]).astype(jnp.bfloat16)
    lists = act_blocks.reshape(row_count, half_blocks, list_width)
    tables, filled = jax.vmap(partial(slot_tables, block_count=lat_count, slot_count=slot_count))(
        lists
    )
    own_table = lax.dynamic_index_in_dim(tables, row_index, 0, keepdims=False)
    own_filled = lax.dynamic_index_in_dim(filled, row_index, 0, keepdims=False)
    mine_filled = lax.dynamic_index_in_dim(filled, lat_index, 1, keepdims=False)
    send_rows = own_table.T
    send_live = own_filled.T
    slot_flags = lax.dynamic_index_in_dim(mine_filled, row_index, 0, keepdims=False)
    wire_shape = (slot_count, block_rows, feature_dim)
    mask_bf = send_live.astype(jnp.bfloat16)[..., None]
    mask_f = send_live.astype(jnp.float32)[..., None]
    back_shape = send_rows.shape + (flat_width,)
    outgoing = (centred[send_rows] * mask_bf).reshape(wire_shape)
    items = lax.all_to_all(outgoing, "lat", split_axis=1, concat_axis=1, tiled=True)
    latent_codes, sigmas, pieces = lax.map(
        lambda bundle: encode_slot(dict_full, bias_full, bundle[0], bundle[1]), (items, slot_flags)
    )
    returned = lax.all_to_all(pieces, "lat", split_axis=1, concat_axis=1, tiled=True)
    returned = returned.reshape(back_shape).astype(jnp.float32) * mask_f
    rebuilt = jnp.zeros((half_blocks, flat_width), jnp.float32).at[send_rows].add(returned)
    errors = (rebuilt - centred.astype(jnp.float32)).astype(jnp.bfloat16)
    err_out = (errors[send_rows] * mask_bf).reshape(wire_shape)
    err_items = lax.all_to_all(err_out, "lat", split_axis=1, concat_axis=1, tiled=True)
    slopes = lax.map(
        lambda bundle: slope_slot(dict_full, bundle[0], bundle[1], bundle[2]),
        (err_items, sigmas, slot_flags),
    )
    total = jnp.einsum("srl,srd->ld", latent_codes, err_items, preferred_element_type=jnp.float32)
    total = total + jnp.einsum("srl,srd->ld", slopes, items, preferred_element_type=jnp.float32)
    grads = lax.psum_scatter(total / block_rows, "row", scatter_dimension=0, tiled=True)
    return grads.astype(jnp.bfloat16)


def after(values, *tokens):
    anywhere = pl.BlockSpec(memory_space=pl.ANY)

    def nothing(*refs):
        del refs

    return pl.pallas_call(
        nothing,
        out_shape=[jax.ShapeDtypeStruct(v.shape, v.dtype) for v in values],
        in_specs=[anywhere] * (len(values) + len(tokens)),
        out_specs=[anywhere] * len(values),
        input_output_aliases={i: i for i in range(len(values))},
        compiler_params=pltpu.CompilerParams(vmem_limit_bytes=2**20),
        cost_estimate=pl.CostEstimate(flops=0, bytes_accessed=0, transcendentals=0),
    )(*values, *tokens)


def local_call(
    kernel, grid, in_specs, out_specs, out_shape, args, aliases=None, scratch=(), cost=(0, 0)
):
    return pl.pallas_call(
        kernel,
        grid=grid,
        in_specs=in_specs,
        out_specs=out_specs,
        out_shape=out_shape,
        scratch_shapes=scratch,
        input_output_aliases=aliases or {},
        compiler_params=pltpu.CompilerParams(vmem_limit_bytes=24 * 2**20),
        cost_estimate=pl.CostEstimate(flops=cost[0], bytes_accessed=cost[1], transcendentals=0),
    )(*args)


def whole(x):
    return pl.BlockSpec(x.shape, lambda i: (0,) * x.ndim)


def columns(x, tile):
    return pl.BlockSpec((x.shape[0], tile), lambda i: (0, i))


def centre(mine, theirs, dec_bias):
    count, width = mine.shape

    def kernel(x_ref, y_ref, b_ref, o_ref):
        shift = b_ref[...].astype(jnp.float32)
        o_ref[:count, :] = (x_ref[...].astype(jnp.float32) - shift).astype(o_ref.dtype)
        o_ref[count:, :] = (y_ref[...].astype(jnp.float32) - shift).astype(o_ref.dtype)

    tile = width // TILES
    out = jax.ShapeDtypeStruct((2 * count, width), jnp.bfloat16)
    args = (mine, theirs, dec_bias)
    return local_call(kernel, (TILES,), [columns(x, tile) for x in args], columns(out, tile), out, args)


def product(x, y, dims):
    return lax.dot_general(x, y, (dims, ((), ())), preferred_element_type=jnp.float32)


def encode(rows, words, bias, listed, which):
    count, tile, n = words[0].shape[0], rows.shape[1] // TILES, len(words)

    def kernel(x_ref, *refs):
        w_refs, (b_ref, m_ref), outs, acc = refs[:n], refs[n : n + 2], refs[n + 2 : -1], refs[-1]

        @pl.when(pl.program_id(0) == 0)
        def _():
            for k, i in enumerate(which):
                row = jnp.broadcast_to(b_ref[i : i + 1, :], (acc.shape[0], count))
                acc[:, k * count : (k + 1) * count] = row

        every = jnp.concatenate([w[...] for w in w_refs]) if n > 1 else w_refs[0][...]
        acc[...] += product(x_ref[...], every, ((1,), (1,)))

        @pl.when(pl.program_id(0) == TILES - 1)
        def _():
            for k, i in enumerate(which):
                p = acc[:, k * count : (k + 1) * count]
                mask = m_ref[:, i : i + 1] > 0
                code = jnp.maximum(p, 0.0) + jnp.log1p(jnp.exp(-jnp.abs(p)))
                outs[2 * k][...] = jnp.where(mask, code, 0.0).astype(jnp.bfloat16)
                outs[2 * k + 1][...] = jnp.where(mask, jax.nn.sigmoid(p), 0.0)

    shape = (rows.shape[0], count)
    out = [jax.ShapeDtypeStruct(shape, t) for _ in words for t in (jnp.bfloat16, jnp.float32)]
    return local_call(
        kernel,
        (TILES,),
        [columns(x, tile) for x in (rows, *words)] + [whole(bias), whole(listed)],
        [whole(o) for o in out],
        out,
        (rows, *words, bias, listed),
        scratch=[pltpu.VMEM((shape[0], n * count), jnp.float32)],
    )


def decode(codes, words, total, dtype):
    n, width = len(words), words[0].shape[1]
    tile = width // TILES

    def kernel(*refs):
        part = None
        for k in range(n):
            one = product(refs[k][...], refs[n + k][...], ((1,), (0,)))
            part = one if part is None else part + one
        rest = refs[2 * n :]
        part = part if len(rest) == 1 else part + rest[0][...]
        rest[-1][...] = part.astype(dtype)

    out = jax.ShapeDtypeStruct((codes[0].shape[0], width), dtype)
    args = (*codes, *words) if total is None else (*codes, *words, total)
    specs = [whole(c) for c in codes] + [columns(w, tile) for w in words]
    specs += [columns(out, tile)] * (len(args) - 2 * n)
    aliases = {2 * n: 0} if total is not None and total.dtype == dtype else None
    return local_call(kernel, (TILES,), specs, columns(out, tile), out, args, aliases)


def slope(errors, words, sigma):
    tile = words.shape[1] // TILES

    def kernel(e_ref, w_ref, s_ref, o_ref, acc):
        @pl.when(pl.program_id(0) == 0)
        def _():
            acc[...] = jnp.zeros_like(acc)

        acc[...] += product(e_ref[...], w_ref[...], ((1,), (1,)))

        @pl.when(pl.program_id(0) == TILES - 1)
        def _():
            o_ref[...] = (acc[...] * s_ref[...]).astype(o_ref.dtype)

    return local_call(
        kernel,
        (TILES,),
        [columns(errors, tile), columns(words, tile), whole(sigma)],
        whole(sigma),
        jax.ShapeDtypeStruct(sigma.shape, jnp.bfloat16),
        (errors, words, sigma),
        scratch=[pltpu.VMEM(sigma.shape, jnp.float32)],
        cost=(2 * sigma.size * words.shape[1], 2 * (errors.size + words.size)),
    )


def gradient(codes, slopes, errors, rows):
    tile = rows.shape[1] // TILES

    def kernel(c_ref, s_ref, e_ref, x_ref, o_ref):
        part = product(c_ref[...], e_ref[...], ((0,), (0,)))
        o_ref[...] = part + product(s_ref[...], x_ref[...], ((0,), (0,)))

    out = jax.ShapeDtypeStruct((codes.shape[1], rows.shape[1]), jnp.float32)
    return local_call(
        kernel,
        (TILES,),
        [whole(codes), whole(slopes), columns(errors, tile), columns(rows, tile)],
        columns(out, tile),
        out,
        (codes, slopes, errors, rows),
        cost=(4 * codes.size * rows.shape[1], 4 * (rows.size + out.size)),
    )


def join(total, came, which):
    count, width = total.shape[0] // 2, total.shape[1]
    tile = width // TILES

    def kernel(*refs):
        value = refs[0][...]
        for ref in refs[1:-1]:
            value = value + ref[...].astype(jnp.float32)
        refs[-1][...] = value.astype(refs[-1].dtype)

    out = jax.ShapeDtypeStruct((count, width), jnp.bfloat16)
    args = (total,) if came is None else (total, came)
    specs = [pl.BlockSpec((count, tile), lambda i: (which, i))]
    specs += [columns(out, tile)] * (len(args) - 1)
    cost = (out.size, 8 * out.size)
    return local_call(kernel, (TILES,), specs, columns(out, tile), out, args, cost=cost)


def ring_body(activations, act_blocks, dictionary, enc_bias, dec_bias):
    count = lax.axis_size("lat")
    lat_index = lax.axis_index("lat")
    row_index = lax.axis_index("row")
    half_blocks, rows_each, width = activations.shape
    latents = dictionary.shape[0]
    cut = latents // 2
    block_rows = rows_each * count
    half = count // 2

    order = list(range(0, count, 2)) + list(range(count - 1, 0, -2))
    right_pairs = [(order[i], order[(i + 1) % count]) for i in range(count)]
    left_pairs = [(b, a) for a, b in right_pairs]
    place = jnp.where(lat_index % 2 == 0, lat_index // 2, count - 1 - lat_index // 2)

    def to_right(x):
        return lax.ppermute(x, "lat", right_pairs)

    def to_left(x):
        return lax.ppermute(x, "lat", left_pairs)

    def to_core(x):
        return lax.ppermute(x, "row", [(0, 1), (1, 0)])

    def owner(step):
        at = (place + step + count) % count
        return jnp.where(at < half, 2 * at, 2 * (count - 1 - at) + 1)

    lists = act_blocks.reshape(2, half_blocks, act_blocks.shape[1])
    lists = jnp.where(row_index == 0, lists, lists[::-1]).reshape(2 * half_blocks, -1)
    steps = [0] + [s for t in range(1, half) for s in (-t, t)] + [half]
    owners = jnp.stack([owner(s) for s in steps])
    listed = jnp.any(lists[:, :, None] == owners, axis=1).astype(jnp.float32)
    listed = jnp.repeat(listed, rows_each, axis=0)

    biases = jnp.broadcast_to(enc_bias.reshape(1, latents), (count, latents))
    biases = lax.all_to_all(biases, "lat", split_axis=0, concat_axis=0, tiled=True)
    pick = (owners[:, None] == jnp.arange(count)).astype(biases.dtype)
    biases = jnp.einsum("so,ol->sl", pick, biases, preferred_element_type=jnp.float32)

    acts = activations.reshape(half_blocks * rows_each, width)
    rows = None

    words = {0: dictionary}
    codes, sigmas, rebuilt = {}, {}, None
    for t in range(1, half):
        arrived = to_right(words[1 - t]), to_left(words[t - 1])
        if t == 1:
            words[-1], words[1] = after(arrived, biases)
            (shift,) = after((dec_bias.reshape(1, width),), words[1])
            rows = centre(acts, to_core(acts), shift)
        else:
            words[-t], words[t] = after(arrived, rebuilt)
        for group in ((-t, t),) if t > 1 else ((0,), (-t, t)):
            blocks = [words[step] for step in group]
            out = encode(rows, blocks, biases, listed, [steps.index(step) for step in group])
            for k, step in enumerate(group):
                codes[step], sigmas[step] = out[2 * k : 2 * k + 2]
            dtype = jnp.bfloat16 if t == half - 1 and group[-1] == t else jnp.float32
            rebuilt = decode([codes[step] for step in group], blocks, rebuilt, dtype)

    middle = half_blocks * rows_each
    swapped = to_core(rebuilt)
    last = to_right(words[1 - half][:cut]), to_left(words[half - 1][cut:])
    last = after(last, rebuilt)
    words[half] = jnp.concatenate(last)
    other_words = to_core(words[half])
    preacts = jnp.einsum("rd,ld->rl", rows, words[half], preferred_element_type=jnp.float32)
    preacts = preacts + biases[-1:]
    mask = listed[:, len(steps) - 1 :] > 0
    code = jnp.where(mask, jax.nn.softplus(preacts), 0.0).astype(jnp.bfloat16)
    sigma = jnp.where(mask, jax.nn.sigmoid(preacts), 0.0)
    codes[half], sigmas[half] = lax.optimization_barrier((code, sigma))
    other_codes = to_core(codes[half])

    def in_my_order(x):
        return jnp.concatenate([x[middle:], x[:middle]])

    errors = rebuilt.astype(jnp.float32) + in_my_order(swapped).astype(jnp.float32)
    errors = errors - rows.astype(jnp.float32)
    for code, word in ((codes[half], words[half]), (in_my_order(other_codes), other_words)):
        errors = errors + jnp.einsum("rl,ld->rd", code, word, preferred_element_type=jnp.float32)
    errors = errors.astype(jnp.bfloat16)

    def grads_of(step, token):
        (sigma,) = after((sigmas[step],), token)
        slopes = slope(errors, words[step], sigma)
        return gradient(codes[step], slopes, errors, rows)

    def send(x):
        return x.astype(jnp.bfloat16)

    slopes = jnp.einsum("rd,ld->rl", errors, words[half], preferred_element_type=jnp.float32)
    slopes = lax.optimization_barrier((slopes * sigmas[half]).astype(jnp.bfloat16))
    far = jnp.einsum("rl,rd->ld", codes[half], errors, preferred_element_type=jnp.float32)
    far = send(far + jnp.einsum("rl,rd->ld", slopes, rows, preferred_element_type=jnp.float32))
    up = (to_right(far[:cut]), None)
    down = (None, to_left(far[cut:]))
    tokens = (far, far)
    for step in range(half - 1, 0, -1):
        ahead, behind = grads_of(step, tokens[0]), grads_of(-step, tokens[1])
        tokens = (up[0], down[1])
        up = tuple(to_right(join(ahead, came, k)) for k, came in enumerate(up))
        down = tuple(to_left(join(behind, came, k)) for k, came in enumerate(down))
    mine = grads_of(0, tokens[0])
    parts = []
    for k in range(2):
        part = mine[k * cut : (k + 1) * cut] + up[k].astype(jnp.float32) + down[k].astype(jnp.float32)
        parts.append(part / block_rows)
    return jnp.concatenate(parts).astype(jnp.bfloat16)


def solution(mesh):
    in_specs = (
        P(("grp", "row"), "lat", None),
        P("grp", None),
        P(("grp", "lat", "row"), None),
        P(("grp", "lat", "row")),
        P("grp"),
    )
    out_specs = P(("grp", "lat", "row"), None)
    lat_count, row_count = mesh.shape["lat"], mesh.shape["row"]

    def body(activations, act_blocks, dictionary, enc_bias, dec_bias):
        gathered = lat_count * dictionary.size * dictionary.dtype.itemsize
        fits = row_count == 2 and lat_count % 2 == 0 and gathered <= GATHER_LIMIT
        step = ring_body if fits else exchange_body
        return step(activations, act_blocks, dictionary, enc_bias, dec_bias)

    return jax.shard_map(body, mesh=mesh, in_specs=in_specs, out_specs=out_specs, check_vma=False)
```

```python
from functools import partial

import jax
import jax.numpy as jnp
from jax import lax
from jax.experimental import pallas as pl
from jax.experimental.pallas import tpu as pltpu
from jax.sharding import PartitionSpec as P

GATHER_LIMIT = 32 * 2**20
TILES = 4


def slot_tables(lists, block_count, slot_count):
    row_total = lists.shape[0]
    labels = jnp.arange(block_count, dtype=jnp.int32)
    matches = jnp.sum((lists[:, :, None] == labels[None, None, :]).astype(jnp.int32), axis=1)
    position = jnp.cumsum(matches, axis=0) - 1
    places = jnp.arange(slot_count, dtype=jnp.int32)
    hits = ((matches[:, :, None] == 1) & (position[:, :, None] == places[None, None, :])).astype(
        jnp.int32
    )
    row_ids = jnp.arange(row_total, dtype=jnp.int32)
    table = jnp.sum(hits * row_ids[:, None, None], axis=0)
    filled = jnp.sum(hits, axis=0)
    return (table, filled)


def encode_slot(dict_full, bias_full, slot_rows, is_filled):
    latent_width = dict_full.shape[0]

    def encode_active(inputs):
        preacts = jnp.einsum("rd,ld->rl", inputs, dict_full, preferred_element_type=jnp.float32)
        preacts = preacts + bias_full.astype(jnp.float32)
        latent_codes = jax.nn.softplus(preacts).astype(jnp.bfloat16)
        pieces = jnp.einsum(
            "rl,ld->rd", latent_codes, dict_full, preferred_element_type=jnp.float32
        )
        return (latent_codes, jax.nn.sigmoid(preacts), pieces.astype(jnp.bfloat16))

    def encode_vacant(inputs):
        return (
            jnp.zeros((inputs.shape[0], latent_width), jnp.bfloat16),
            jnp.zeros((inputs.shape[0], latent_width), jnp.float32),
            jnp.zeros_like(inputs),
        )

    return lax.cond(is_filled > 0, encode_active, encode_vacant, slot_rows)


def slope_slot(dict_full, err_rows, sigmas, is_filled):

    def slope_active(err_in, sig_in):
        code_grads = jnp.einsum("rd,ld->rl", err_in, dict_full, preferred_element_type=jnp.float32)
        return (code_grads * sig_in).astype(jnp.bfloat16)

    def slope_vacant(err_in, sig_in):
        return jnp.zeros(sig_in.shape, jnp.bfloat16)

    return lax.cond(is_filled > 0, slope_active, slope_vacant, err_rows, sigmas)


def exchange_body(activations, act_blocks, dictionary, enc_bias, dec_bias):
    lat_count = lax.axis_size("lat")
    row_count = lax.axis_size("row")
    lat_index = lax.axis_index("lat")
    row_index = lax.axis_index("row")
    half_blocks, rows_each, feature_dim = activations.shape
    list_width = act_blocks.shape[1]
    slot_count = list_width * half_blocks // lat_count
    block_rows = rows_each * lat_count
    flat_width = rows_each * feature_dim
    dict_full, bias_full = (
        lax.all_gather(dictionary, "row", axis=0, tiled=True),
        lax.all_gather(enc_bias, "row", axis=0, tiled=True),
    )
    flat_acts = activations.reshape(half_blocks, flat_width)
    bias_flat = jnp.tile(dec_bias.astype(jnp.float32), rows_each)
    centred = (flat_acts.astype(jnp.float32) - bias_flat[None, :]).astype(jnp.bfloat16)
    lists = act_blocks.reshape(row_count, half_blocks, list_width)
    tables, filled = jax.vmap(partial(slot_tables, block_count=lat_count, slot_count=slot_count))(
        lists
    )
    own_table = lax.dynamic_index_in_dim(tables, row_index, 0, keepdims=False)
    own_filled = lax.dynamic_index_in_dim(filled, row_index, 0, keepdims=False)
    mine_filled = lax.dynamic_index_in_dim(filled, lat_index, 1, keepdims=False)
    send_rows = own_table.T
    send_live = own_filled.T
    slot_flags = lax.dynamic_index_in_dim(mine_filled, row_index, 0, keepdims=False)
    wire_shape = (slot_count, block_rows, feature_dim)
    mask_bf = send_live.astype(jnp.bfloat16)[..., None]
    mask_f = send_live.astype(jnp.float32)[..., None]
    back_shape = send_rows.shape + (flat_width,)
    outgoing = (centred[send_rows] * mask_bf).reshape(wire_shape)
    items = lax.all_to_all(outgoing, "lat", split_axis=1, concat_axis=1, tiled=True)
    latent_codes, sigmas, pieces = lax.map(
        lambda bundle: encode_slot(dict_full, bias_full, bundle[0], bundle[1]), (items, slot_flags)
    )
    returned = lax.all_to_all(pieces, "lat", split_axis=1, concat_axis=1, tiled=True)
    returned = returned.reshape(back_shape).astype(jnp.float32) * mask_f
    rebuilt = jnp.zeros((half_blocks, flat_width), jnp.float32).at[send_rows].add(returned)
    errors = (rebuilt - centred.astype(jnp.float32)).astype(jnp.bfloat16)
    err_out = (errors[send_rows] * mask_bf).reshape(wire_shape)
    err_items = lax.all_to_all(err_out, "lat", split_axis=1, concat_axis=1, tiled=True)
    slopes = lax.map(
        lambda bundle: slope_slot(dict_full, bundle[0], bundle[1], bundle[2]),
        (err_items, sigmas, slot_flags),
    )
    total = jnp.einsum("srl,srd->ld", latent_codes, err_items, preferred_element_type=jnp.float32)
    total = total + jnp.einsum("srl,srd->ld", slopes, items, preferred_element_type=jnp.float32)
    grads = lax.psum_scatter(total / block_rows, "row", scatter_dimension=0, tiled=True)
    return grads.astype(jnp.bfloat16)


def after(values, *tokens):
    anywhere = pl.BlockSpec(memory_space=pl.ANY)

    def nothing(*refs):
        del refs

    return pl.pallas_call(
        nothing,
        out_shape=[jax.ShapeDtypeStruct(v.shape, v.dtype) for v in values],
        in_specs=[anywhere] * (len(values) + len(tokens)),
        out_specs=[anywhere] * len(values),
        input_output_aliases={i: i for i in range(len(values))},
        compiler_params=pltpu.CompilerParams(vmem_limit_bytes=2**20),
        cost_estimate=pl.CostEstimate(flops=0, bytes_accessed=0, transcendentals=0),
    )(*values, *tokens)


def local_call(
    kernel, grid, in_specs, out_specs, out_shape, args, aliases=None, scratch=(), cost=(0, 0)
):
    return pl.pallas_call(
        kernel,
        grid=grid,
        in_specs=in_specs,
        out_specs=out_specs,
        out_shape=out_shape,
        scratch_shapes=scratch,
        input_output_aliases=aliases or {},
        compiler_params=pltpu.CompilerParams(vmem_limit_bytes=24 * 2**20),
        cost_estimate=pl.CostEstimate(flops=cost[0], bytes_accessed=cost[1], transcendentals=0),
    )(*args)


def whole(x):
    return pl.BlockSpec(x.shape, lambda i: (0,) * x.ndim)


def columns(x, tile):
    return pl.BlockSpec((x.shape[0], tile), lambda i: (0, i))


def centre(mine, theirs, dec_bias):
    count, width = mine.shape

    def kernel(x_ref, y_ref, b_ref, o_ref):
        shift = b_ref[...].astype(jnp.float32)
        o_ref[:count, :] = (x_ref[...].astype(jnp.float32) - shift).astype(o_ref.dtype)
        o_ref[count:, :] = (y_ref[...].astype(jnp.float32) - shift).astype(o_ref.dtype)

    tile = width // TILES
    out = jax.ShapeDtypeStruct((2 * count, width), jnp.bfloat16)
    args = (mine, theirs, dec_bias)
    return local_call(kernel, (TILES,), [columns(x, tile) for x in args], columns(out, tile), out, args)


def product(x, y, dims):
    return lax.dot_general(x, y, (dims, ((), ())), preferred_element_type=jnp.float32)


def encode(rows, words, biases, listed, which):
    count, tile, n = words[0].shape[0], rows.shape[1] // TILES, len(words)

    def kernel(x_ref, *refs):
        w_refs, b_refs, m_ref = refs[:n], refs[n : 2 * n], refs[2 * n]
        outs, acc = refs[2 * n + 1 : -1], refs[-1]

        @pl.when(pl.program_id(0) == 0)
        def _():
            for k in range(n):
                row = jnp.broadcast_to(b_refs[k][...].astype(jnp.float32), (acc.shape[0], count))
                acc[:, k * count : (k + 1) * count] = row

        every = jnp.concatenate([w[...] for w in w_refs]) if n > 1 else w_refs[0][...]
        acc[...] += product(x_ref[...], every, ((1,), (1,)))

        @pl.when(pl.program_id(0) == TILES - 1)
        def _():
            for k, i in enumerate(which):
                p = acc[:, k * count : (k + 1) * count]
                mask = m_ref[:, i : i + 1] > 0
                code = jnp.maximum(p, 0.0) + jnp.log1p(jnp.exp(-jnp.abs(p)))
                outs[2 * k][...] = jnp.where(mask, code, 0.0).astype(jnp.bfloat16)
                outs[2 * k + 1][...] = jnp.where(mask, jax.nn.sigmoid(p), 0.0)

    shape = (rows.shape[0], count)
    out = [jax.ShapeDtypeStruct(shape, t) for _ in words for t in (jnp.bfloat16, jnp.float32)]
    return local_call(
        kernel,
        (TILES,),
        [columns(x, tile) for x in (rows, *words)] + [whole(x) for x in (*biases, listed)],
        [whole(o) for o in out],
        out,
        (rows, *words, *biases, listed),
        scratch=[pltpu.VMEM((shape[0], n * count), jnp.float32)],
    )


def decode(codes, words, total, dtype):
    n, width = len(words), words[0].shape[1]
    tile = width // TILES

    def kernel(*refs):
        part = None
        for k in range(n):
            one = product(refs[k][...], refs[n + k][...], ((1,), (0,)))
            part = one if part is None else part + one
        rest = refs[2 * n :]
        part = part if len(rest) == 1 else part + rest[0][...]
        rest[-1][...] = part.astype(dtype)

    out = jax.ShapeDtypeStruct((codes[0].shape[0], width), dtype)
    args = (*codes, *words) if total is None else (*codes, *words, total)
    specs = [whole(c) for c in codes] + [columns(w, tile) for w in words]
    specs += [columns(out, tile)] * (len(args) - 2 * n)
    aliases = {2 * n: 0} if total is not None and total.dtype == dtype else None
    return local_call(kernel, (TILES,), specs, columns(out, tile), out, args, aliases)


def slope(errors, words, sigma):
    tile = words.shape[1] // TILES

    def kernel(e_ref, w_ref, s_ref, o_ref, acc):
        @pl.when(pl.program_id(0) == 0)
        def _():
            acc[...] = jnp.zeros_like(acc)

        acc[...] += product(e_ref[...], w_ref[...], ((1,), (1,)))

        @pl.when(pl.program_id(0) == TILES - 1)
        def _():
            o_ref[...] = (acc[...] * s_ref[...]).astype(o_ref.dtype)

    return local_call(
        kernel,
        (TILES,),
        [columns(errors, tile), columns(words, tile), whole(sigma)],
        whole(sigma),
        jax.ShapeDtypeStruct(sigma.shape, jnp.bfloat16),
        (errors, words, sigma),
        scratch=[pltpu.VMEM(sigma.shape, jnp.float32)],
        cost=(2 * sigma.size * words.shape[1], 2 * (errors.size + words.size)),
    )


def gradient(codes, slopes, errors, rows):
    tile = rows.shape[1] // TILES

    def kernel(c_ref, s_ref, e_ref, x_ref, o_ref):
        part = product(c_ref[...], e_ref[...], ((0,), (0,)))
        o_ref[...] = part + product(s_ref[...], x_ref[...], ((0,), (0,)))

    out = jax.ShapeDtypeStruct((codes.shape[1], rows.shape[1]), jnp.float32)
    return local_call(
        kernel,
        (TILES,),
        [whole(codes), whole(slopes), columns(errors, tile), columns(rows, tile)],
        columns(out, tile),
        out,
        (codes, slopes, errors, rows),
        cost=(4 * codes.size * rows.shape[1], 4 * (rows.size + out.size)),
    )


def join(total, came, which):
    count, width = total.shape[0] // 2, total.shape[1]
    tile = width // TILES

    def kernel(*refs):
        value = refs[0][...]
        for ref in refs[1:-1]:
            value = value + ref[...].astype(jnp.float32)
        refs[-1][...] = value.astype(refs[-1].dtype)

    out = jax.ShapeDtypeStruct((count, width), jnp.bfloat16)
    args = (total,) if came is None else (total, came)
    specs = [pl.BlockSpec((count, tile), lambda i: (which, i))]
    specs += [columns(out, tile)] * (len(args) - 1)
    cost = (out.size, 8 * out.size)
    return local_call(kernel, (TILES,), specs, columns(out, tile), out, args, cost=cost)


def ring_body(activations, act_blocks, dictionary, enc_bias, dec_bias):
    count = lax.axis_size("lat")
    lat_index = lax.axis_index("lat")
    row_index = lax.axis_index("row")
    half_blocks, rows_each, width = activations.shape
    latents = dictionary.shape[0]
    cut = latents // 2
    block_rows = rows_each * count
    half = count // 2

    order = list(range(0, count, 2)) + list(range(count - 1, 0, -2))
    right_pairs = [(order[i], order[(i + 1) % count]) for i in range(count)]
    left_pairs = [(b, a) for a, b in right_pairs]
    place = jnp.where(lat_index % 2 == 0, lat_index // 2, count - 1 - lat_index // 2)

    def to_right(x):
        return lax.ppermute(x, "lat", right_pairs)

    def to_left(x):
        return lax.ppermute(x, "lat", left_pairs)

    def to_core(x):
        return lax.ppermute(x, "row", [(0, 1), (1, 0)])

    def owner(step):
        at = (place + step + count) % count
        return jnp.where(at < half, 2 * at, 2 * (count - 1 - at) + 1)

    lists = act_blocks.reshape(2, half_blocks, act_blocks.shape[1])
    lists = jnp.where(row_index == 0, lists, lists[::-1]).reshape(2 * half_blocks, -1)
    steps = [0] + [s for t in range(1, half) for s in (-t, t)] + [half]
    owners = jnp.stack([owner(s) for s in steps])
    listed = jnp.any(lists[:, :, None] == owners, axis=1).astype(jnp.float32)
    listed = jnp.repeat(listed, rows_each, axis=0)

    acts = activations.reshape(half_blocks * rows_each, width)
    rows = None

    words, biases = {0: dictionary}, {0: enc_bias.reshape(1, latents)}
    codes, sigmas, rebuilt = {}, {}, None
    for t in range(1, half):
        arrived = to_right(words[1 - t]), to_left(words[t - 1])
        small = to_right(biases[1 - t]), to_left(biases[t - 1])
        tokens = () if rebuilt is None else (rebuilt,)
        words[-t], words[t], biases[-t], biases[t] = after((*arrived, *small), *tokens)
        if t == 1:
            (shift,) = after((dec_bias.reshape(1, width),), words[1])
            rows = centre(acts, to_core(acts), shift)
        for group in ((-t, t),) if t > 1 else ((0,), (-t, t)):
            blocks = [words[step] for step in group]
            shifts = [biases[step] for step in group]
            out = encode(rows, blocks, shifts, listed, [steps.index(step) for step in group])
            for k, step in enumerate(group):
                codes[step], sigmas[step] = out[2 * k : 2 * k + 2]
            dtype = jnp.bfloat16 if t == half - 1 and group[-1] == t else jnp.float32
            rebuilt = decode([codes[step] for step in group], blocks, rebuilt, dtype)

    middle = half_blocks * rows_each
    swapped = to_core(rebuilt)
    last = to_right(words[1 - half][:cut]), to_left(words[half - 1][cut:])
    *last, biases[half] = after((*last, to_right(biases[1 - half])), rebuilt)
    words[half] = jnp.concatenate(last)
    other_words = to_core(words[half])
    preacts = jnp.einsum("rd,ld->rl", rows, words[half], preferred_element_type=jnp.float32)
    preacts = preacts + biases[half].astype(jnp.float32)
    mask = listed[:, len(steps) - 1 :] > 0
    code = jnp.where(mask, jax.nn.softplus(preacts), 0.0).astype(jnp.bfloat16)
    sigma = jnp.where(mask, jax.nn.sigmoid(preacts), 0.0)
    codes[half], sigmas[half] = lax.optimization_barrier((code, sigma))
    other_codes = to_core(codes[half])

    def in_my_order(x):
        return jnp.concatenate([x[middle:], x[:middle]])

    errors = rebuilt.astype(jnp.float32) + in_my_order(swapped).astype(jnp.float32)
    errors = errors - rows.astype(jnp.float32)
    for code, word in ((codes[half], words[half]), (in_my_order(other_codes), other_words)):
        errors = errors + jnp.einsum("rl,ld->rd", code, word, preferred_element_type=jnp.float32)
    errors = errors.astype(jnp.bfloat16)

    def grads_of(step, token):
        (sigma,) = after((sigmas[step],), token)
        slopes = slope(errors, words[step], sigma)
        return gradient(codes[step], slopes, errors, rows)

    def send(x):
        return x.astype(jnp.bfloat16)

    slopes = jnp.einsum("rd,ld->rl", errors, words[half], preferred_element_type=jnp.float32)
    slopes = lax.optimization_barrier((slopes * sigmas[half]).astype(jnp.bfloat16))
    far = jnp.einsum("rl,rd->ld", codes[half], errors, preferred_element_type=jnp.float32)
    far = send(far + jnp.einsum("rl,rd->ld", slopes, rows, preferred_element_type=jnp.float32))
    up = (to_right(far[:cut]), None)
    down = (None, to_left(far[cut:]))
    tokens = (far, far)
    for step in range(half - 1, 0, -1):
        ahead, behind = grads_of(step, tokens[0]), grads_of(-step, tokens[1])
        tokens = (up[0], down[1])
        up = tuple(to_right(join(ahead, came, k)) for k, came in enumerate(up))
        down = tuple(to_left(join(behind, came, k)) for k, came in enumerate(down))
    mine = grads_of(0, tokens[0])
    parts = []
    for k in range(2):
        part = mine[k * cut : (k + 1) * cut] + up[k].astype(jnp.float32) + down[k].astype(jnp.float32)
        parts.append(part / block_rows)
    return jnp.concatenate(parts).astype(jnp.bfloat16)


def solution(mesh):
    in_specs = (
        P(("grp", "row"), "lat", None),
        P("grp", None),
        P(("grp", "lat", "row"), None),
        P(("grp", "lat", "row")),
        P("grp"),
    )
    out_specs = P(("grp", "lat", "row"), None)
    lat_count, row_count = mesh.shape["lat"], mesh.shape["row"]

    def body(activations, act_blocks, dictionary, enc_bias, dec_bias):
        gathered = lat_count * dictionary.size * dictionary.dtype.itemsize
        fits = row_count == 2 and lat_count % 2 == 0 and gathered <= GATHER_LIMIT
        step = ring_body if fits else exchange_body
        return step(activations, act_blocks, dictionary, enc_bias, dec_bias)

    return jax.shard_map(body, mesh=mesh, in_specs=in_specs, out_specs=out_specs, check_vma=False)
```

```python
from functools import partial

import jax
import jax.numpy as jnp
from jax import lax
from jax.experimental import pallas as pl
from jax.experimental.pallas import tpu as pltpu
from jax.sharding import PartitionSpec as P

GATHER_LIMIT = 32 * 2**20
TILES = 4


def slot_tables(lists, block_count, slot_count):
    row_total = lists.shape[0]
    labels = jnp.arange(block_count, dtype=jnp.int32)
    matches = jnp.sum((lists[:, :, None] == labels[None, None, :]).astype(jnp.int32), axis=1)
    position = jnp.cumsum(matches, axis=0) - 1
    places = jnp.arange(slot_count, dtype=jnp.int32)
    hits = ((matches[:, :, None] == 1) & (position[:, :, None] == places[None, None, :])).astype(
        jnp.int32
    )
    row_ids = jnp.arange(row_total, dtype=jnp.int32)
    table = jnp.sum(hits * row_ids[:, None, None], axis=0)
    filled = jnp.sum(hits, axis=0)
    return (table, filled)


def encode_slot(dict_full, bias_full, slot_rows, is_filled):
    latent_width = dict_full.shape[0]

    def encode_active(inputs):
        preacts = jnp.einsum("rd,ld->rl", inputs, dict_full, preferred_element_type=jnp.float32)
        preacts = preacts + bias_full.astype(jnp.float32)
        latent_codes = jax.nn.softplus(preacts).astype(jnp.bfloat16)
        pieces = jnp.einsum(
            "rl,ld->rd", latent_codes, dict_full, preferred_element_type=jnp.float32
        )
        return (latent_codes, jax.nn.sigmoid(preacts), pieces.astype(jnp.bfloat16))

    def encode_vacant(inputs):
        return (
            jnp.zeros((inputs.shape[0], latent_width), jnp.bfloat16),
            jnp.zeros((inputs.shape[0], latent_width), jnp.float32),
            jnp.zeros_like(inputs),
        )

    return lax.cond(is_filled > 0, encode_active, encode_vacant, slot_rows)


def slope_slot(dict_full, err_rows, sigmas, is_filled):

    def slope_active(err_in, sig_in):
        code_grads = jnp.einsum("rd,ld->rl", err_in, dict_full, preferred_element_type=jnp.float32)
        return (code_grads * sig_in).astype(jnp.bfloat16)

    def slope_vacant(err_in, sig_in):
        return jnp.zeros(sig_in.shape, jnp.bfloat16)

    return lax.cond(is_filled > 0, slope_active, slope_vacant, err_rows, sigmas)


def exchange_body(activations, act_blocks, dictionary, enc_bias, dec_bias):
    lat_count = lax.axis_size("lat")
    row_count = lax.axis_size("row")
    lat_index = lax.axis_index("lat")
    row_index = lax.axis_index("row")
    half_blocks, rows_each, feature_dim = activations.shape
    list_width = act_blocks.shape[1]
    slot_count = list_width * half_blocks // lat_count
    block_rows = rows_each * lat_count
    flat_width = rows_each * feature_dim
    dict_full, bias_full = (
        lax.all_gather(dictionary, "row", axis=0, tiled=True),
        lax.all_gather(enc_bias, "row", axis=0, tiled=True),
    )
    flat_acts = activations.reshape(half_blocks, flat_width)
    bias_flat = jnp.tile(dec_bias.astype(jnp.float32), rows_each)
    centred = (flat_acts.astype(jnp.float32) - bias_flat[None, :]).astype(jnp.bfloat16)
    lists = act_blocks.reshape(row_count, half_blocks, list_width)
    tables, filled = jax.vmap(partial(slot_tables, block_count=lat_count, slot_count=slot_count))(
        lists
    )
    own_table = lax.dynamic_index_in_dim(tables, row_index, 0, keepdims=False)
    own_filled = lax.dynamic_index_in_dim(filled, row_index, 0, keepdims=False)
    mine_filled = lax.dynamic_index_in_dim(filled, lat_index, 1, keepdims=False)
    send_rows = own_table.T
    send_live = own_filled.T
    slot_flags = lax.dynamic_index_in_dim(mine_filled, row_index, 0, keepdims=False)
    wire_shape = (slot_count, block_rows, feature_dim)
    mask_bf = send_live.astype(jnp.bfloat16)[..., None]
    mask_f = send_live.astype(jnp.float32)[..., None]
    back_shape = send_rows.shape + (flat_width,)
    outgoing = (centred[send_rows] * mask_bf).reshape(wire_shape)
    items = lax.all_to_all(outgoing, "lat", split_axis=1, concat_axis=1, tiled=True)
    latent_codes, sigmas, pieces = lax.map(
        lambda bundle: encode_slot(dict_full, bias_full, bundle[0], bundle[1]), (items, slot_flags)
    )
    returned = lax.all_to_all(pieces, "lat", split_axis=1, concat_axis=1, tiled=True)
    returned = returned.reshape(back_shape).astype(jnp.float32) * mask_f
    rebuilt = jnp.zeros((half_blocks, flat_width), jnp.float32).at[send_rows].add(returned)
    errors = (rebuilt - centred.astype(jnp.float32)).astype(jnp.bfloat16)
    err_out = (errors[send_rows] * mask_bf).reshape(wire_shape)
    err_items = lax.all_to_all(err_out, "lat", split_axis=1, concat_axis=1, tiled=True)
    slopes = lax.map(
        lambda bundle: slope_slot(dict_full, bundle[0], bundle[1], bundle[2]),
        (err_items, sigmas, slot_flags),
    )
    total = jnp.einsum("srl,srd->ld", latent_codes, err_items, preferred_element_type=jnp.float32)
    total = total + jnp.einsum("srl,srd->ld", slopes, items, preferred_element_type=jnp.float32)
    grads = lax.psum_scatter(total / block_rows, "row", scatter_dimension=0, tiled=True)
    return grads.astype(jnp.bfloat16)


def after(values, *tokens):
    anywhere = pl.BlockSpec(memory_space=pl.ANY)

    def nothing(*refs):
        del refs

    return pl.pallas_call(
        nothing,
        out_shape=[jax.ShapeDtypeStruct(v.shape, v.dtype) for v in values],
        in_specs=[anywhere] * (len(values) + len(tokens)),
        out_specs=[anywhere] * len(values),
        input_output_aliases={i: i for i in range(len(values))},
        compiler_params=pltpu.CompilerParams(vmem_limit_bytes=2**20),
        cost_estimate=pl.CostEstimate(flops=0, bytes_accessed=0, transcendentals=0),
    )(*values, *tokens)


def local_call(
    kernel, grid, in_specs, out_specs, out_shape, args, aliases=None, scratch=(), cost=(0, 0)
):
    return pl.pallas_call(
        kernel,
        grid=grid,
        in_specs=in_specs,
        out_specs=out_specs,
        out_shape=out_shape,
        scratch_shapes=scratch,
        input_output_aliases=aliases or {},
        compiler_params=pltpu.CompilerParams(vmem_limit_bytes=24 * 2**20),
        cost_estimate=pl.CostEstimate(flops=cost[0], bytes_accessed=cost[1], transcendentals=0),
    )(*args)


def whole(x):
    return pl.BlockSpec(x.shape, lambda i: (0,) * x.ndim)


def columns(x, tile):
    return pl.BlockSpec((x.shape[0], tile), lambda i: (0, i))


def centre(mine, theirs, dec_bias):
    count, width = mine.shape

    def kernel(x_ref, y_ref, b_ref, o_ref):
        shift = b_ref[...].astype(jnp.float32)
        o_ref[:count, :] = (x_ref[...].astype(jnp.float32) - shift).astype(o_ref.dtype)
        o_ref[count:, :] = (y_ref[...].astype(jnp.float32) - shift).astype(o_ref.dtype)

    tile = width // TILES
    out = jax.ShapeDtypeStruct((2 * count, width), jnp.bfloat16)
    args = (mine, theirs, dec_bias)
    return local_call(kernel, (TILES,), [columns(x, tile) for x in args], columns(out, tile), out, args)


def product(x, y, dims):
    return lax.dot_general(x, y, (dims, ((), ())), preferred_element_type=jnp.float32)


def encode(rows, words, biases, listed, which):
    count, tile, n = words[0].shape[0], rows.shape[1] // TILES, len(words)

    def kernel(x_ref, *refs):
        w_refs, b_refs, m_ref = refs[:n], refs[n : 2 * n], refs[2 * n]
        outs, acc = refs[2 * n + 1 : -1], refs[-1]

        @pl.when(pl.program_id(0) == 0)
        def _():
            for k in range(n):
                row = jnp.broadcast_to(b_refs[k][...].astype(jnp.float32), (acc.shape[0], count))
                acc[:, k * count : (k + 1) * count] = row

        every = jnp.concatenate([w[...] for w in w_refs]) if n > 1 else w_refs[0][...]
        acc[...] += product(x_ref[...], every, ((1,), (1,)))

        @pl.when(pl.program_id(0) == TILES - 1)
        def _():
            for k, i in enumerate(which):
                p = acc[:, k * count : (k + 1) * count]
                mask = m_ref[:, i : i + 1] > 0
                code = jnp.maximum(p, 0.0) + jnp.log1p(jnp.exp(-jnp.abs(p)))
                outs[2 * k][...] = jnp.where(mask, code, 0.0).astype(jnp.bfloat16)
                outs[2 * k + 1][...] = jnp.where(mask, jax.nn.sigmoid(p), 0.0)

    shape = (rows.shape[0], count)
    out = [jax.ShapeDtypeStruct(shape, t) for _ in words for t in (jnp.bfloat16, jnp.float32)]
    return local_call(
        kernel,
        (TILES,),
        [columns(x, tile) for x in (rows, *words)] + [whole(x) for x in (*biases, listed)],
        [whole(o) for o in out],
        out,
        (rows, *words, *biases, listed),
        scratch=[pltpu.VMEM((shape[0], n * count), jnp.float32)],
    )


def decode(codes, words, total, dtype):
    n, width = len(words), words[0].shape[1]
    tile = width // TILES

    def kernel(*refs):
        part = None
        for k in range(n):
            one = product(refs[k][...], refs[n + k][...], ((1,), (0,)))
            part = one if part is None else part + one
        rest = refs[2 * n :]
        part = part if len(rest) == 1 else part + rest[0][...]
        rest[-1][...] = part.astype(dtype)

    out = jax.ShapeDtypeStruct((codes[0].shape[0], width), dtype)
    args = (*codes, *words) if total is None else (*codes, *words, total)
    specs = [whole(c) for c in codes] + [columns(w, tile) for w in words]
    specs += [columns(out, tile)] * (len(args) - 2 * n)
    aliases = {2 * n: 0} if total is not None and total.dtype == dtype else None
    return local_call(kernel, (TILES,), specs, columns(out, tile), out, args, aliases)


def slope(errors, words, sigma):
    tile = words.shape[1] // TILES

    def kernel(e_ref, w_ref, s_ref, o_ref, acc):
        @pl.when(pl.program_id(0) == 0)
        def _():
            acc[...] = jnp.zeros_like(acc)

        acc[...] += product(e_ref[...], w_ref[...], ((1,), (1,)))

        @pl.when(pl.program_id(0) == TILES - 1)
        def _():
            o_ref[...] = (acc[...] * s_ref[...]).astype(o_ref.dtype)

    return local_call(
        kernel,
        (TILES,),
        [columns(errors, tile), columns(words, tile), whole(sigma)],
        whole(sigma),
        jax.ShapeDtypeStruct(sigma.shape, jnp.bfloat16),
        (errors, words, sigma),
        scratch=[pltpu.VMEM(sigma.shape, jnp.float32)],
        cost=(2 * sigma.size * words.shape[1], 2 * (errors.size + words.size)),
    )


def gradient(codes, slopes, errors, rows):
    tile = rows.shape[1] // TILES

    def kernel(c_ref, s_ref, e_ref, x_ref, o_ref):
        part = product(c_ref[...], e_ref[...], ((0,), (0,)))
        o_ref[...] = part + product(s_ref[...], x_ref[...], ((0,), (0,)))

    out = jax.ShapeDtypeStruct((codes.shape[1], rows.shape[1]), jnp.float32)
    return local_call(
        kernel,
        (TILES,),
        [whole(codes), whole(slopes), columns(errors, tile), columns(rows, tile)],
        columns(out, tile),
        out,
        (codes, slopes, errors, rows),
        cost=(4 * codes.size * rows.shape[1], 4 * (rows.size + out.size)),
    )


def join(total, came, which):
    count, width = total.shape[0] // 2, total.shape[1]
    tile = width // TILES

    def kernel(*refs):
        value = refs[0][...]
        for ref in refs[1:-1]:
            value = value + ref[...].astype(jnp.float32)
        refs[-1][...] = value.astype(refs[-1].dtype)

    out = jax.ShapeDtypeStruct((count, width), jnp.bfloat16)
    args = (total,) if came is None else (total, came)
    specs = [pl.BlockSpec((count, tile), lambda i: (which, i))]
    specs += [columns(out, tile)] * (len(args) - 1)
    cost = (out.size, 8 * out.size)
    return local_call(kernel, (TILES,), specs, columns(out, tile), out, args, cost=cost)


def ring_body(activations, act_blocks, dictionary, enc_bias, dec_bias):
    count = lax.axis_size("lat")
    lat_index = lax.axis_index("lat")
    row_index = lax.axis_index("row")
    half_blocks, rows_each, width = activations.shape
    latents = dictionary.shape[0]
    cut = latents // 2
    block_rows = rows_each * count
    half = count // 2

    order = list(range(0, count, 2)) + list(range(count - 1, 0, -2))
    right_pairs = [(order[i], order[(i + 1) % count]) for i in range(count)]
    left_pairs = [(b, a) for a, b in right_pairs]
    place = jnp.where(lat_index % 2 == 0, lat_index // 2, count - 1 - lat_index // 2)

    def to_right(x):
        return lax.ppermute(x, "lat", right_pairs)

    def to_left(x):
        return lax.ppermute(x, "lat", left_pairs)

    def to_core(x):
        return lax.ppermute(x, "row", [(0, 1), (1, 0)])

    def owner(step):
        at = (place + step + count) % count
        return jnp.where(at < half, 2 * at, 2 * (count - 1 - at) + 1)

    lists = act_blocks.reshape(2, half_blocks, act_blocks.shape[1])
    lists = jnp.where(row_index == 0, lists, lists[::-1]).reshape(2 * half_blocks, -1)
    steps = [0] + [s for t in range(1, half) for s in (-t, t)] + [half]
    owners = jnp.stack([owner(s) for s in steps])
    listed = jnp.any(lists[:, :, None] == owners, axis=1).astype(jnp.float32)
    listed = jnp.repeat(listed, rows_each, axis=0)

    acts = activations.reshape(half_blocks * rows_each, width)
    rows = None

    words, biases = {0: dictionary}, {0: enc_bias.reshape(1, latents)}
    codes, sigmas, rebuilt = {}, {}, None
    for t in range(1, half):
        arrived = to_right(words[1 - t]), to_left(words[t - 1])
        small = to_right(biases[1 - t]), to_left(biases[t - 1])
        tokens = () if rebuilt is None else (rebuilt,)
        words[-t], biases[-t] = after((arrived[0], small[0]), *tokens)
        words[t], biases[t] = after((arrived[1], small[1]), *tokens)
        if t == 1:
            (shift,) = after((dec_bias.reshape(1, width),), words[1])
            rows = centre(acts, to_core(acts), shift)
        for group in ((-t, t),) if t > 1 else ((0,), (-t, t)):
            blocks = [words[step] for step in group]
            shifts = [biases[step] for step in group]
            out = encode(rows, blocks, shifts, listed, [steps.index(step) for step in group])
            for k, step in enumerate(group):
                codes[step], sigmas[step] = out[2 * k : 2 * k + 2]
            dtype = jnp.bfloat16 if t == half - 1 and group[-1] == t else jnp.float32
            rebuilt = decode([codes[step] for step in group], blocks, rebuilt, dtype)

    middle = half_blocks * rows_each
    swapped = to_core(rebuilt)
    last = to_right(words[1 - half][:cut]), to_left(words[half - 1][cut:])
    *last, biases[half] = after((*last, to_right(biases[1 - half])), rebuilt)
    words[half] = jnp.concatenate(last)
    other_words = to_core(words[half])
    preacts = jnp.einsum("rd,ld->rl", rows, words[half], preferred_element_type=jnp.float32)
    preacts = preacts + biases[half].astype(jnp.float32)
    mask = listed[:, len(steps) - 1 :] > 0
    code = jnp.where(mask, jax.nn.softplus(preacts), 0.0).astype(jnp.bfloat16)
    sigma = jnp.where(mask, jax.nn.sigmoid(preacts), 0.0)
    codes[half], sigmas[half] = lax.optimization_barrier((code, sigma))
    other_codes = to_core(codes[half])

    def in_my_order(x):
        return jnp.concatenate([x[middle:], x[:middle]])

    errors = rebuilt.astype(jnp.float32) + in_my_order(swapped).astype(jnp.float32)
    errors = errors - rows.astype(jnp.float32)
    for code, word in ((codes[half], words[half]), (in_my_order(other_codes), other_words)):
        errors = errors + jnp.einsum("rl,ld->rd", code, word, preferred_element_type=jnp.float32)
    errors = errors.astype(jnp.bfloat16)

    def grads_of(step, token):
        (sigma,) = after((sigmas[step],), token)
        slopes = slope(errors, words[step], sigma)
        return gradient(codes[step], slopes, errors, rows)

    def send(x):
        return x.astype(jnp.bfloat16)

    slopes = jnp.einsum("rd,ld->rl", errors, words[half], preferred_element_type=jnp.float32)
    slopes = lax.optimization_barrier((slopes * sigmas[half]).astype(jnp.bfloat16))
    far = jnp.einsum("rl,rd->ld", codes[half], errors, preferred_element_type=jnp.float32)
    far = send(far + jnp.einsum("rl,rd->ld", slopes, rows, preferred_element_type=jnp.float32))
    up = (to_right(far[:cut]), None)
    down = (None, to_left(far[cut:]))
    tokens = (far, far)
    for step in range(half - 1, 0, -1):
        ahead, behind = grads_of(step, tokens[0]), grads_of(-step, tokens[1])
        tokens = (up[0], down[1])
        up = tuple(to_right(join(ahead, came, k)) for k, came in enumerate(up))
        down = tuple(to_left(join(behind, came, k)) for k, came in enumerate(down))
    mine = grads_of(0, tokens[0])
    parts = []
    for k in range(2):
        part = mine[k * cut : (k + 1) * cut] + up[k].astype(jnp.float32) + down[k].astype(jnp.float32)
        parts.append(part / block_rows)
    return jnp.concatenate(parts).astype(jnp.bfloat16)


def solution(mesh):
    in_specs = (
        P(("grp", "row"), "lat", None),
        P("grp", None),
        P(("grp", "lat", "row"), None),
        P(("grp", "lat", "row")),
        P("grp"),
    )
    out_specs = P(("grp", "lat", "row"), None)
    lat_count, row_count = mesh.shape["lat"], mesh.shape["row"]

    def body(activations, act_blocks, dictionary, enc_bias, dec_bias):
        gathered = lat_count * dictionary.size * dictionary.dtype.itemsize
        fits = row_count == 2 and lat_count % 2 == 0 and gathered <= GATHER_LIMIT
        step = ring_body if fits else exchange_body
        return step(activations, act_blocks, dictionary, enc_bias, dec_bias)

    return jax.shard_map(body, mesh=mesh, in_specs=in_specs, out_specs=out_specs, check_vma=False)
```

```python
from functools import partial

import jax
import jax.numpy as jnp
from jax import lax
from jax.experimental import pallas as pl
from jax.experimental.pallas import tpu as pltpu
from jax.sharding import PartitionSpec as P

GATHER_LIMIT = 32 * 2**20
TILES = 2


def slot_tables(lists, block_count, slot_count):
    row_total = lists.shape[0]
    labels = jnp.arange(block_count, dtype=jnp.int32)
    matches = jnp.sum((lists[:, :, None] == labels[None, None, :]).astype(jnp.int32), axis=1)
    position = jnp.cumsum(matches, axis=0) - 1
    places = jnp.arange(slot_count, dtype=jnp.int32)
    hits = ((matches[:, :, None] == 1) & (position[:, :, None] == places[None, None, :])).astype(
        jnp.int32
    )
    row_ids = jnp.arange(row_total, dtype=jnp.int32)
    table = jnp.sum(hits * row_ids[:, None, None], axis=0)
    filled = jnp.sum(hits, axis=0)
    return (table, filled)


def encode_slot(dict_full, bias_full, slot_rows, is_filled):
    latent_width = dict_full.shape[0]

    def encode_active(inputs):
        preacts = jnp.einsum("rd,ld->rl", inputs, dict_full, preferred_element_type=jnp.float32)
        preacts = preacts + bias_full.astype(jnp.float32)
        latent_codes = jax.nn.softplus(preacts).astype(jnp.bfloat16)
        pieces = jnp.einsum(
            "rl,ld->rd", latent_codes, dict_full, preferred_element_type=jnp.float32
        )
        return (latent_codes, jax.nn.sigmoid(preacts), pieces.astype(jnp.bfloat16))

    def encode_vacant(inputs):
        return (
            jnp.zeros((inputs.shape[0], latent_width), jnp.bfloat16),
            jnp.zeros((inputs.shape[0], latent_width), jnp.float32),
            jnp.zeros_like(inputs),
        )

    return lax.cond(is_filled > 0, encode_active, encode_vacant, slot_rows)


def slope_slot(dict_full, err_rows, sigmas, is_filled):

    def slope_active(err_in, sig_in):
        code_grads = jnp.einsum("rd,ld->rl", err_in, dict_full, preferred_element_type=jnp.float32)
        return (code_grads * sig_in).astype(jnp.bfloat16)

    def slope_vacant(err_in, sig_in):
        return jnp.zeros(sig_in.shape, jnp.bfloat16)

    return lax.cond(is_filled > 0, slope_active, slope_vacant, err_rows, sigmas)


def exchange_body(activations, act_blocks, dictionary, enc_bias, dec_bias):
    lat_count = lax.axis_size("lat")
    row_count = lax.axis_size("row")
    lat_index = lax.axis_index("lat")
    row_index = lax.axis_index("row")
    half_blocks, rows_each, feature_dim = activations.shape
    list_width = act_blocks.shape[1]
    slot_count = list_width * half_blocks // lat_count
    block_rows = rows_each * lat_count
    flat_width = rows_each * feature_dim
    dict_full, bias_full = (
        lax.all_gather(dictionary, "row", axis=0, tiled=True),
        lax.all_gather(enc_bias, "row", axis=0, tiled=True),
    )
    flat_acts = activations.reshape(half_blocks, flat_width)
    bias_flat = jnp.tile(dec_bias.astype(jnp.float32), rows_each)
    centred = (flat_acts.astype(jnp.float32) - bias_flat[None, :]).astype(jnp.bfloat16)
    lists = act_blocks.reshape(row_count, half_blocks, list_width)
    tables, filled = jax.vmap(partial(slot_tables, block_count=lat_count, slot_count=slot_count))(
        lists
    )
    own_table = lax.dynamic_index_in_dim(tables, row_index, 0, keepdims=False)
    own_filled = lax.dynamic_index_in_dim(filled, row_index, 0, keepdims=False)
    mine_filled = lax.dynamic_index_in_dim(filled, lat_index, 1, keepdims=False)
    send_rows = own_table.T
    send_live = own_filled.T
    slot_flags = lax.dynamic_index_in_dim(mine_filled, row_index, 0, keepdims=False)
    wire_shape = (slot_count, block_rows, feature_dim)
    mask_bf = send_live.astype(jnp.bfloat16)[..., None]
    mask_f = send_live.astype(jnp.float32)[..., None]
    back_shape = send_rows.shape + (flat_width,)
    outgoing = (centred[send_rows] * mask_bf).reshape(wire_shape)
    items = lax.all_to_all(outgoing, "lat", split_axis=1, concat_axis=1, tiled=True)
    latent_codes, sigmas, pieces = lax.map(
        lambda bundle: encode_slot(dict_full, bias_full, bundle[0], bundle[1]), (items, slot_flags)
    )
    returned = lax.all_to_all(pieces, "lat", split_axis=1, concat_axis=1, tiled=True)
    returned = returned.reshape(back_shape).astype(jnp.float32) * mask_f
    rebuilt = jnp.zeros((half_blocks, flat_width), jnp.float32).at[send_rows].add(returned)
    errors = (rebuilt - centred.astype(jnp.float32)).astype(jnp.bfloat16)
    err_out = (errors[send_rows] * mask_bf).reshape(wire_shape)
    err_items = lax.all_to_all(err_out, "lat", split_axis=1, concat_axis=1, tiled=True)
    slopes = lax.map(
        lambda bundle: slope_slot(dict_full, bundle[0], bundle[1], bundle[2]),
        (err_items, sigmas, slot_flags),
    )
    total = jnp.einsum("srl,srd->ld", latent_codes, err_items, preferred_element_type=jnp.float32)
    total = total + jnp.einsum("srl,srd->ld", slopes, items, preferred_element_type=jnp.float32)
    grads = lax.psum_scatter(total / block_rows, "row", scatter_dimension=0, tiled=True)
    return grads.astype(jnp.bfloat16)


def after(values, *tokens):
    anywhere = pl.BlockSpec(memory_space=pl.ANY)

    def nothing(*refs):
        del refs

    return pl.pallas_call(
        nothing,
        out_shape=[jax.ShapeDtypeStruct(v.shape, v.dtype) for v in values],
        in_specs=[anywhere] * (len(values) + len(tokens)),
        out_specs=[anywhere] * len(values),
        input_output_aliases={i: i for i in range(len(values))},
        compiler_params=pltpu.CompilerParams(vmem_limit_bytes=2**20),
        cost_estimate=pl.CostEstimate(flops=0, bytes_accessed=0, transcendentals=0),
    )(*values, *tokens)


def local_call(
    kernel, grid, in_specs, out_specs, out_shape, args, aliases=None, scratch=(), cost=(0, 0)
):
    return pl.pallas_call(
        kernel,
        grid=grid,
        in_specs=in_specs,
        out_specs=out_specs,
        out_shape=out_shape,
        scratch_shapes=scratch,
        input_output_aliases=aliases or {},
        compiler_params=pltpu.CompilerParams(vmem_limit_bytes=24 * 2**20),
        cost_estimate=pl.CostEstimate(flops=cost[0], bytes_accessed=cost[1], transcendentals=0),
    )(*args)


def whole(x):
    return pl.BlockSpec(x.shape, lambda i: (0,) * x.ndim)


def columns(x, tile):
    return pl.BlockSpec((x.shape[0], tile), lambda i: (0, i))


def centre(mine, theirs, dec_bias, first):
    count, width = mine.shape

    def kernel(x_ref, y_ref, b_ref, f_ref, o_ref):
        shift = b_ref[...].astype(jnp.float32)
        x, y = (r[...].astype(jnp.float32) - shift for r in (x_ref, y_ref))
        mask = f_ref[:, :1] > 0
        o_ref[:count, :] = jnp.where(mask, x, y).astype(o_ref.dtype)
        o_ref[count:, :] = jnp.where(mask, y, x).astype(o_ref.dtype)

    tile = width // TILES
    out = jax.ShapeDtypeStruct((2 * count, width), jnp.bfloat16)
    args = (mine, theirs, dec_bias, first)
    specs = [columns(x, tile) for x in args[:3]] + [whole(first)]
    return local_call(kernel, (TILES,), specs, columns(out, tile), out, args)


def product(x, y, dims):
    return lax.dot_general(x, y, (dims, ((), ())), preferred_element_type=jnp.float32)


def encode(rows, words, biases, listed, which):
    count, tile, n = words[0].shape[0], rows.shape[1] // TILES, len(words)

    def kernel(x_ref, *refs):
        w_refs, b_refs, m_ref = refs[:n], refs[n : 2 * n], refs[2 * n]
        outs, acc = refs[2 * n + 1 : -1], refs[-1]

        @pl.when(pl.program_id(0) == 0)
        def _():
            for k in range(n):
                row = jnp.broadcast_to(b_refs[k][...].astype(jnp.float32), (acc.shape[0], count))
                acc[:, k * count : (k + 1) * count] = row

        every = jnp.concatenate([w[...] for w in w_refs]) if n > 1 else w_refs[0][...]
        acc[...] += product(x_ref[...], every, ((1,), (1,)))

        @pl.when(pl.program_id(0) == TILES - 1)
        def _():
            for k, i in enumerate(which):
                p = acc[:, k * count : (k + 1) * count]
                mask = m_ref[:, i : i + 1] > 0
                code = jnp.maximum(p, 0.0) + jnp.log1p(jnp.exp(-jnp.abs(p)))
                outs[2 * k][...] = jnp.where(mask, code, 0.0).astype(jnp.bfloat16)
                outs[2 * k + 1][...] = jnp.where(mask, jax.nn.sigmoid(p), 0.0)

    shape = (rows.shape[0], count)
    out = [jax.ShapeDtypeStruct(shape, t) for _ in words for t in (jnp.bfloat16, jnp.float32)]
    return local_call(
        kernel,
        (TILES,),
        [columns(x, tile) for x in (rows, *words)] + [whole(x) for x in (*biases, listed)],
        [whole(o) for o in out],
        out,
        (rows, *words, *biases, listed),
        scratch=[pltpu.VMEM((shape[0], n * count), jnp.float32)],
    )


def decode(codes, words, total, dtype):
    n, width = len(words), words[0].shape[1]
    tile = width // TILES

    def kernel(*refs):
        part = None
        for k in range(n):
            one = product(refs[k][...], refs[n + k][...], ((1,), (0,)))
            part = one if part is None else part + one
        rest = refs[2 * n :]
        part = part if len(rest) == 1 else part + rest[0][...]
        rest[-1][...] = part.astype(dtype)

    out = jax.ShapeDtypeStruct((codes[0].shape[0], width), dtype)
    args = (*codes, *words) if total is None else (*codes, *words, total)
    specs = [whole(c) for c in codes] + [columns(w, tile) for w in words]
    specs += [columns(out, tile)] * (len(args) - 2 * n)
    aliases = {2 * n: 0} if total is not None and total.dtype == dtype else None
    return local_call(kernel, (TILES,), specs, columns(out, tile), out, args, aliases)


def slope(errors, words, sigma):
    tile = words.shape[1] // TILES

    def kernel(e_ref, w_ref, s_ref, o_ref, acc):
        @pl.when(pl.program_id(0) == 0)
        def _():
            acc[...] = jnp.zeros_like(acc)

        acc[...] += product(e_ref[...], w_ref[...], ((1,), (1,)))

        @pl.when(pl.program_id(0) == TILES - 1)
        def _():
            o_ref[...] = (acc[...] * s_ref[...]).astype(o_ref.dtype)

    return local_call(
        kernel,
        (TILES,),
        [columns(errors, tile), columns(words, tile), whole(sigma)],
        whole(sigma),
        jax.ShapeDtypeStruct(sigma.shape, jnp.bfloat16),
        (errors, words, sigma),
        scratch=[pltpu.VMEM(sigma.shape, jnp.float32)],
        cost=(2 * sigma.size * words.shape[1], 2 * (errors.size + words.size)),
    )


def gradient(codes, slopes, errors, rows):
    tile = rows.shape[1] // TILES

    def kernel(c_ref, s_ref, e_ref, x_ref, o_ref):
        part = product(c_ref[...], e_ref[...], ((0,), (0,)))
        o_ref[...] = part + product(s_ref[...], x_ref[...], ((0,), (0,)))

    out = jax.ShapeDtypeStruct((codes.shape[1], rows.shape[1]), jnp.float32)
    return local_call(
        kernel,
        (TILES,),
        [whole(codes), whole(slopes), columns(errors, tile), columns(rows, tile)],
        columns(out, tile),
        out,
        (codes, slopes, errors, rows),
        cost=(4 * codes.size * rows.shape[1], 4 * (rows.size + out.size)),
    )


def join(total, came, which):
    count, width = total.shape[0] // 2, total.shape[1]
    tile = width // TILES

    def kernel(*refs):
        value = refs[0][...]
        for ref in refs[1:-1]:
            value = value + ref[...].astype(jnp.float32)
        refs[-1][...] = value.astype(refs[-1].dtype)

    out = jax.ShapeDtypeStruct((count, width), jnp.bfloat16)
    args = (total,) if came is None else (total, came)
    specs = [pl.BlockSpec((count, tile), lambda i: (which, i))]
    specs += [columns(out, tile)] * (len(args) - 1)
    cost = (out.size, 8 * out.size)
    return local_call(kernel, (TILES,), specs, columns(out, tile), out, args, cost=cost)


def ring_body(activations, act_blocks, dictionary, enc_bias, dec_bias):
    count = lax.axis_size("lat")
    lat_index = lax.axis_index("lat")
    row_index = lax.axis_index("row")
    half_blocks, rows_each, width = activations.shape
    latents = dictionary.shape[0]
    cut = latents // 2
    block_rows = rows_each * count
    half = count // 2

    order = list(range(0, count, 2)) + list(range(count - 1, 0, -2))
    right_pairs = [(order[i], order[(i + 1) % count]) for i in range(count)]
    left_pairs = [(b, a) for a, b in right_pairs]
    place = jnp.where(lat_index % 2 == 0, lat_index // 2, count - 1 - lat_index // 2)

    def to_right(x):
        return lax.ppermute(x, "lat", right_pairs)

    def to_left(x):
        return lax.ppermute(x, "lat", left_pairs)

    def to_core(x):
        return lax.ppermute(x, "row", [(0, 1), (1, 0)])

    def owner(step):
        at = (place + step + count) % count
        return jnp.where(at < half, 2 * at, 2 * (count - 1 - at) + 1)

    lists = act_blocks
    core_0 = jnp.broadcast_to((row_index == 0).astype(jnp.float32), (1, 128))
    steps = [0] + [s for t in range(1, half) for s in (-t, t)] + [half]
    owners = jnp.stack([owner(s) for s in steps])
    listed = jnp.any(lists[:, :, None] == owners, axis=1).astype(jnp.float32)
    listed = jnp.repeat(listed, rows_each, axis=0)

    acts = activations.reshape(half_blocks * rows_each, width)
    rows = None

    words, biases = {0: dictionary}, {0: enc_bias.reshape(1, latents)}
    codes, sigmas, rebuilt = {}, {}, None
    for t in range(1, half):
        arrived = to_right(words[1 - t]), to_left(words[t - 1])
        small = to_right(biases[1 - t]), to_left(biases[t - 1])
        tokens = () if rebuilt is None else (rebuilt,)
        words[-t], biases[-t] = after((arrived[0], small[0]), *tokens)
        if t < half - 1:
            words[t], biases[t] = after((arrived[1], small[1]), *tokens)
        else:
            opposite = [(order[i], order[(i + half) % count]) for i in range(count)]
            far_bias = lax.ppermute(biases[0], "lat", opposite)
            words[t], biases[t], biases[half] = after((arrived[1], small[1], far_bias), *tokens)
        if t == 1:
            (shift,) = after((dec_bias.reshape(1, width),), words[1])
            rows = centre(acts, to_core(acts), shift, core_0)
        for group in ((-t, t),) if t > 1 else ((0,), (-t, t)):
            blocks = [words[step] for step in group]
            shifts = [biases[step] for step in group]
            out = encode(rows, blocks, shifts, listed, [steps.index(step) for step in group])
            for k, step in enumerate(group):
                codes[step], sigmas[step] = out[2 * k : 2 * k + 2]
            dtype = jnp.bfloat16 if t == half - 1 and group[-1] == t else jnp.float32
            rebuilt = decode([codes[step] for step in group], blocks, rebuilt, dtype)

    swapped = to_core(rebuilt)
    last = to_right(words[1 - half][:cut]), to_left(words[half - 1][cut:])
    last = after(last, rebuilt)
    words[half] = jnp.concatenate(last)
    other_words = to_core(words[half])
    preacts = jnp.einsum("rd,ld->rl", rows, words[half], preferred_element_type=jnp.float32)
    preacts = preacts + biases[half].astype(jnp.float32)
    mask = listed[:, len(steps) - 1 :] > 0
    code = jnp.where(mask, jax.nn.softplus(preacts), 0.0).astype(jnp.bfloat16)
    sigma = jnp.where(mask, jax.nn.sigmoid(preacts), 0.0)
    codes[half], sigmas[half] = lax.optimization_barrier((code, sigma))
    other_codes = to_core(codes[half])

    errors = rebuilt.astype(jnp.float32) + swapped.astype(jnp.float32)
    errors = errors - rows.astype(jnp.float32)
    for code, word in ((codes[half], words[half]), (other_codes, other_words)):
        errors = errors + jnp.einsum("rl,ld->rd", code, word, preferred_element_type=jnp.float32)
    errors = errors.astype(jnp.bfloat16)

    def grads_of(step, token):
        (sigma,) = after((sigmas[step],), token)
        slopes = slope(errors, words[step], sigma)
        return gradient(codes[step], slopes, errors, rows)

    def send(x):
        return x.astype(jnp.bfloat16)

    slopes = jnp.einsum("rd,ld->rl", errors, words[half], preferred_element_type=jnp.float32)
    slopes = lax.optimization_barrier((slopes * sigmas[half]).astype(jnp.bfloat16))
    far = jnp.einsum("rl,rd->ld", codes[half], errors, preferred_element_type=jnp.float32)
    far = send(far + jnp.einsum("rl,rd->ld", slopes, rows, preferred_element_type=jnp.float32))
    up = (to_right(far[:cut]), None)
    down = (None, to_left(far[cut:]))
    tokens = (far, far)
    for step in range(half - 1, 0, -1):
        ahead, behind = grads_of(step, tokens[0]), grads_of(-step, tokens[1])
        tokens = (up[0], down[1])
        up = tuple(to_right(join(ahead, came, k)) for k, came in enumerate(up))
        down = tuple(to_left(join(behind, came, k)) for k, came in enumerate(down))
    mine = grads_of(0, tokens[0])
    for came in (up, down):
        mine = mine + jnp.concatenate(came).astype(jnp.float32)
    return (mine / block_rows).astype(jnp.bfloat16)


def solution(mesh):
    in_specs = (
        P(("grp", "row"), "lat", None),
        P("grp", None),
        P(("grp", "lat", "row"), None),
        P(("grp", "lat", "row")),
        P("grp"),
    )
    out_specs = P(("grp", "lat", "row"), None)
    lat_count, row_count = mesh.shape["lat"], mesh.shape["row"]

    def body(activations, act_blocks, dictionary, enc_bias, dec_bias):
        gathered = lat_count * dictionary.size * dictionary.dtype.itemsize
        fits = row_count == 2 and lat_count % 2 == 0 and gathered <= GATHER_LIMIT
        step = ring_body if fits else exchange_body
        return step(activations, act_blocks, dictionary, enc_bias, dec_bias)

    return jax.shard_map(body, mesh=mesh, in_specs=in_specs, out_specs=out_specs, check_vma=False)
```

```python
from functools import partial

import jax
import jax.numpy as jnp
from jax import lax
from jax.experimental import pallas as pl
from jax.experimental.pallas import tpu as pltpu
from jax.sharding import PartitionSpec as P

GATHER_LIMIT = 32 * 2**20
TILES = 2


def slot_tables(lists, block_count, slot_count):
    row_total = lists.shape[0]
    labels = jnp.arange(block_count, dtype=jnp.int32)
    matches = jnp.sum((lists[:, :, None] == labels[None, None, :]).astype(jnp.int32), axis=1)
    position = jnp.cumsum(matches, axis=0) - 1
    places = jnp.arange(slot_count, dtype=jnp.int32)
    hits = ((matches[:, :, None] == 1) & (position[:, :, None] == places[None, None, :])).astype(
        jnp.int32
    )
    row_ids = jnp.arange(row_total, dtype=jnp.int32)
    table = jnp.sum(hits * row_ids[:, None, None], axis=0)
    filled = jnp.sum(hits, axis=0)
    return (table, filled)


def encode_slot(dict_full, bias_full, slot_rows, is_filled):
    latent_width = dict_full.shape[0]

    def encode_active(inputs):
        preacts = jnp.einsum("rd,ld->rl", inputs, dict_full, preferred_element_type=jnp.float32)
        preacts = preacts + bias_full.astype(jnp.float32)
        latent_codes = jax.nn.softplus(preacts).astype(jnp.bfloat16)
        pieces = jnp.einsum(
            "rl,ld->rd", latent_codes, dict_full, preferred_element_type=jnp.float32
        )
        return (latent_codes, jax.nn.sigmoid(preacts), pieces.astype(jnp.bfloat16))

    def encode_vacant(inputs):
        return (
            jnp.zeros((inputs.shape[0], latent_width), jnp.bfloat16),
            jnp.zeros((inputs.shape[0], latent_width), jnp.float32),
            jnp.zeros_like(inputs),
        )

    return lax.cond(is_filled > 0, encode_active, encode_vacant, slot_rows)


def slope_slot(dict_full, err_rows, sigmas, is_filled):

    def slope_active(err_in, sig_in):
        code_grads = jnp.einsum("rd,ld->rl", err_in, dict_full, preferred_element_type=jnp.float32)
        return (code_grads * sig_in).astype(jnp.bfloat16)

    def slope_vacant(err_in, sig_in):
        return jnp.zeros(sig_in.shape, jnp.bfloat16)

    return lax.cond(is_filled > 0, slope_active, slope_vacant, err_rows, sigmas)


def exchange_body(activations, act_blocks, dictionary, enc_bias, dec_bias):
    lat_count = lax.axis_size("lat")
    row_count = lax.axis_size("row")
    lat_index = lax.axis_index("lat")
    row_index = lax.axis_index("row")
    half_blocks, rows_each, feature_dim = activations.shape
    list_width = act_blocks.shape[1]
    slot_count = list_width * half_blocks // lat_count
    block_rows = rows_each * lat_count
    flat_width = rows_each * feature_dim
    dict_full, bias_full = (
        lax.all_gather(dictionary, "row", axis=0, tiled=True),
        lax.all_gather(enc_bias, "row", axis=0, tiled=True),
    )
    flat_acts = activations.reshape(half_blocks, flat_width)
    bias_flat = jnp.tile(dec_bias.astype(jnp.float32), rows_each)
    centred = (flat_acts.astype(jnp.float32) - bias_flat[None, :]).astype(jnp.bfloat16)
    lists = act_blocks.reshape(row_count, half_blocks, list_width)
    tables, filled = jax.vmap(partial(slot_tables, block_count=lat_count, slot_count=slot_count))(
        lists
    )
    own_table = lax.dynamic_index_in_dim(tables, row_index, 0, keepdims=False)
    own_filled = lax.dynamic_index_in_dim(filled, row_index, 0, keepdims=False)
    mine_filled = lax.dynamic_index_in_dim(filled, lat_index, 1, keepdims=False)
    send_rows = own_table.T
    send_live = own_filled.T
    slot_flags = lax.dynamic_index_in_dim(mine_filled, row_index, 0, keepdims=False)
    wire_shape = (slot_count, block_rows, feature_dim)
    mask_bf = send_live.astype(jnp.bfloat16)[..., None]
    mask_f = send_live.astype(jnp.float32)[..., None]
    back_shape = send_rows.shape + (flat_width,)
    outgoing = (centred[send_rows] * mask_bf).reshape(wire_shape)
    items = lax.all_to_all(outgoing, "lat", split_axis=1, concat_axis=1, tiled=True)
    latent_codes, sigmas, pieces = lax.map(
        lambda bundle: encode_slot(dict_full, bias_full, bundle[0], bundle[1]), (items, slot_flags)
    )
    returned = lax.all_to_all(pieces, "lat", split_axis=1, concat_axis=1, tiled=True)
    returned = returned.reshape(back_shape).astype(jnp.float32) * mask_f
    rebuilt = jnp.zeros((half_blocks, flat_width), jnp.float32).at[send_rows].add(returned)
    errors = (rebuilt - centred.astype(jnp.float32)).astype(jnp.bfloat16)
    err_out = (errors[send_rows] * mask_bf).reshape(wire_shape)
    err_items = lax.all_to_all(err_out, "lat", split_axis=1, concat_axis=1, tiled=True)
    slopes = lax.map(
        lambda bundle: slope_slot(dict_full, bundle[0], bundle[1], bundle[2]),
        (err_items, sigmas, slot_flags),
    )
    total = jnp.einsum("srl,srd->ld", latent_codes, err_items, preferred_element_type=jnp.float32)
    total = total + jnp.einsum("srl,srd->ld", slopes, items, preferred_element_type=jnp.float32)
    grads = lax.psum_scatter(total / block_rows, "row", scatter_dimension=0, tiled=True)
    return grads.astype(jnp.bfloat16)


def after(values, *tokens):
    anywhere = pl.BlockSpec(memory_space=pl.ANY)

    def nothing(*refs):
        del refs

    return pl.pallas_call(
        nothing,
        out_shape=[jax.ShapeDtypeStruct(v.shape, v.dtype) for v in values],
        in_specs=[anywhere] * (len(values) + len(tokens)),
        out_specs=[anywhere] * len(values),
        input_output_aliases={i: i for i in range(len(values))},
        compiler_params=pltpu.CompilerParams(vmem_limit_bytes=2**20),
        cost_estimate=pl.CostEstimate(flops=0, bytes_accessed=0, transcendentals=0),
    )(*values, *tokens)


def local_call(
    kernel, grid, in_specs, out_specs, out_shape, args, aliases=None, scratch=(), cost=(0, 0)
):
    return pl.pallas_call(
        kernel,
        grid=grid,
        in_specs=in_specs,
        out_specs=out_specs,
        out_shape=out_shape,
        scratch_shapes=scratch,
        input_output_aliases=aliases or {},
        compiler_params=pltpu.CompilerParams(vmem_limit_bytes=24 * 2**20),
        cost_estimate=pl.CostEstimate(flops=cost[0], bytes_accessed=cost[1], transcendentals=0),
    )(*args)


def whole(x):
    return pl.BlockSpec(x.shape, lambda i: (0,) * x.ndim)


def columns(x, tile):
    return pl.BlockSpec((x.shape[0], tile), lambda i: (0, i))


def centre(mine, theirs, dec_bias, first):
    count, width = mine.shape

    def kernel(x_ref, y_ref, b_ref, f_ref, o_ref):
        shift = b_ref[...].astype(jnp.float32)
        x, y = (r[...].astype(jnp.float32) - shift for r in (x_ref, y_ref))
        mask = f_ref[:, :1] > 0
        o_ref[:count, :] = jnp.where(mask, x, y).astype(o_ref.dtype)
        o_ref[count:, :] = jnp.where(mask, y, x).astype(o_ref.dtype)

    tile = width // TILES
    out = jax.ShapeDtypeStruct((2 * count, width), jnp.bfloat16)
    args = (mine, theirs, dec_bias, first)
    specs = [columns(x, tile) for x in args[:3]] + [whole(first)]
    return local_call(kernel, (TILES,), specs, columns(out, tile), out, args)


def product(x, y, dims):
    return lax.dot_general(x, y, (dims, ((), ())), preferred_element_type=jnp.float32)


def encode(rows, words, biases, listed, which):
    count, tile, n = words[0].shape[0], rows.shape[1] // TILES, len(words)

    def kernel(x_ref, *refs):
        w_refs, b_refs, m_ref = refs[:n], refs[n : 2 * n], refs[2 * n]
        outs, acc = refs[2 * n + 1 : -1], refs[-1]

        @pl.when(pl.program_id(0) == 0)
        def _():
            for k in range(n):
                row = jnp.broadcast_to(b_refs[k][...].astype(jnp.float32), (acc.shape[0], count))
                acc[:, k * count : (k + 1) * count] = row

        every = jnp.concatenate([w[...] for w in w_refs]) if n > 1 else w_refs[0][...]
        acc[...] += product(x_ref[...], every, ((1,), (1,)))

        @pl.when(pl.program_id(0) == TILES - 1)
        def _():
            for k, i in enumerate(which):
                p = acc[:, k * count : (k + 1) * count]
                mask = m_ref[:, i : i + 1] > 0
                code = jnp.maximum(p, 0.0) + jnp.log1p(jnp.exp(-jnp.abs(p)))
                outs[2 * k][...] = jnp.where(mask, code, 0.0).astype(jnp.bfloat16)
                outs[2 * k + 1][...] = jnp.where(mask, jax.nn.sigmoid(p), 0.0)

    shape = (rows.shape[0], count)
    out = [jax.ShapeDtypeStruct(shape, t) for _ in words for t in (jnp.bfloat16, jnp.float32)]
    return local_call(
        kernel,
        (TILES,),
        [columns(x, tile) for x in (rows, *words)] + [whole(x) for x in (*biases, listed)],
        [whole(o) for o in out],
        out,
        (rows, *words, *biases, listed),
        scratch=[pltpu.VMEM((shape[0], n * count), jnp.float32)],
    )


def decode(codes, words, total, dtype, rows=None):
    n, width = len(words), words[0].shape[1]
    tile = width // TILES

    def kernel(*refs):
        part = None
        for k in range(n):
            one = product(refs[k][...], refs[n + k][...], ((1,), (0,)))
            part = one if part is None else part + one
        rest = refs[2 * n :]
        part = part if len(rest) == 1 else part + rest[0][...]
        if rows is not None:
            part = part - 0.5 * rest[1][...].astype(jnp.float32)
        rest[-1][...] = part.astype(dtype)

    out = jax.ShapeDtypeStruct((codes[0].shape[0], width), dtype)
    args = (*codes, *words) if total is None else (*codes, *words, total)
    args += () if rows is None else (rows,)
    specs = [whole(c) for c in codes] + [columns(w, tile) for w in words]
    specs += [columns(out, tile)] * (len(args) - 2 * n)
    aliases = {2 * n: 0} if total is not None and total.dtype == dtype else None
    return local_call(kernel, (TILES,), specs, columns(out, tile), out, args, aliases)


def slope(errors, words, sigma):
    tile = words.shape[1] // TILES

    def kernel(e_ref, w_ref, s_ref, o_ref, acc):
        @pl.when(pl.program_id(0) == 0)
        def _():
            acc[...] = jnp.zeros_like(acc)

        acc[...] += product(e_ref[...], w_ref[...], ((1,), (1,)))

        @pl.when(pl.program_id(0) == TILES - 1)
        def _():
            o_ref[...] = (acc[...] * s_ref[...]).astype(o_ref.dtype)

    return local_call(
        kernel,
        (TILES,),
        [columns(errors, tile), columns(words, tile), whole(sigma)],
        whole(sigma),
        jax.ShapeDtypeStruct(sigma.shape, jnp.bfloat16),
        (errors, words, sigma),
        scratch=[pltpu.VMEM(sigma.shape, jnp.float32)],
        cost=(2 * sigma.size * words.shape[1], 2 * (errors.size + words.size)),
    )


def gradient(codes, slopes, errors, rows):
    tile = rows.shape[1] // TILES

    def kernel(c_ref, s_ref, e_ref, x_ref, o_ref):
        part = product(c_ref[...], e_ref[...], ((0,), (0,)))
        o_ref[...] = part + product(s_ref[...], x_ref[...], ((0,), (0,)))

    out = jax.ShapeDtypeStruct((codes.shape[1], rows.shape[1]), jnp.float32)
    return local_call(
        kernel,
        (TILES,),
        [whole(codes), whole(slopes), columns(errors, tile), columns(rows, tile)],
        columns(out, tile),
        out,
        (codes, slopes, errors, rows),
        cost=(4 * codes.size * rows.shape[1], 4 * (rows.size + out.size)),
    )


def join(total, came, which):
    count, width = total.shape[0] // 2, total.shape[1]
    tile = width // TILES

    def kernel(*refs):
        value = refs[0][...]
        for ref in refs[1:-1]:
            value = value + ref[...].astype(jnp.float32)
        refs[-1][...] = value.astype(refs[-1].dtype)

    out = jax.ShapeDtypeStruct((count, width), jnp.bfloat16)
    args = (total,) if came is None else (total, came)
    specs = [pl.BlockSpec((count, tile), lambda i: (which, i))]
    specs += [columns(out, tile)] * (len(args) - 1)
    cost = (out.size, 8 * out.size)
    return local_call(kernel, (TILES,), specs, columns(out, tile), out, args, cost=cost)


def ring_body(activations, act_blocks, dictionary, enc_bias, dec_bias):
    count = lax.axis_size("lat")
    lat_index = lax.axis_index("lat")
    row_index = lax.axis_index("row")
    half_blocks, rows_each, width = activations.shape
    latents = dictionary.shape[0]
    cut = latents // 2
    block_rows = rows_each * count
    half = count // 2

    order = list(range(0, count, 2)) + list(range(count - 1, 0, -2))
    right_pairs = [(order[i], order[(i + 1) % count]) for i in range(count)]
    left_pairs = [(b, a) for a, b in right_pairs]
    place = jnp.where(lat_index % 2 == 0, lat_index // 2, count - 1 - lat_index // 2)

    def to_right(x):
        return lax.ppermute(x, "lat", right_pairs)

    def to_left(x):
        return lax.ppermute(x, "lat", left_pairs)

    def to_core(x):
        return lax.ppermute(x, "row", [(0, 1), (1, 0)])

    def owner(step):
        at = (place + step + count) % count
        return jnp.where(at < half, 2 * at, 2 * (count - 1 - at) + 1)

    lists = act_blocks
    core_0 = jnp.broadcast_to((row_index == 0).astype(jnp.float32), (1, 128))
    steps = [0] + [s for t in range(1, half) for s in (-t, t)] + [half]
    owners = jnp.stack([owner(s) for s in steps])
    listed = jnp.any(lists[:, :, None] == owners, axis=1).astype(jnp.float32)
    listed = jnp.repeat(listed, rows_each, axis=0)

    acts = activations.reshape(half_blocks * rows_each, width)
    rows = None

    words, biases = {0: dictionary}, {0: enc_bias.reshape(1, latents)}
    codes, sigmas, rebuilt = {}, {}, None
    for t in range(1, half):
        arrived = to_right(words[1 - t]), to_left(words[t - 1])
        small = to_right(biases[1 - t]), to_left(biases[t - 1])
        tokens = () if rebuilt is None else (rebuilt,)
        words[-t], biases[-t] = after((arrived[0], small[0]), *tokens)
        if t < half - 1:
            words[t], biases[t] = after((arrived[1], small[1]), *tokens)
        else:
            opposite = [(order[i], order[(i + half) % count]) for i in range(count)]
            far_bias = lax.ppermute(biases[0], "lat", opposite)
            words[t], biases[t], biases[half] = after((arrived[1], small[1], far_bias), *tokens)
        if t == 1:
            (shift,) = after((dec_bias.reshape(1, width),), words[1])
            rows = centre(acts, to_core(acts), shift, core_0)
        for group in ((-t, t),) if t > 1 else ((0,), (-t, t)):
            blocks = [words[step] for step in group]
            shifts = [biases[step] for step in group]
            out = encode(rows, blocks, shifts, listed, [steps.index(step) for step in group])
            for k, step in enumerate(group):
                codes[step], sigmas[step] = out[2 * k : 2 * k + 2]
            final = t == half - 1 and group[-1] == t
            dtype, less = (jnp.bfloat16, rows) if final else (jnp.float32, None)
            rebuilt = decode([codes[step] for step in group], blocks, rebuilt, dtype, less)

    swapped = to_core(rebuilt)
    last = to_right(words[1 - half][:cut]), to_left(words[half - 1][cut:])
    last = after(last, rebuilt)
    words[half] = jnp.concatenate(last)
    other_words = to_core(words[half])
    preacts = jnp.einsum("rd,ld->rl", rows, words[half], preferred_element_type=jnp.float32)
    preacts = preacts + biases[half].astype(jnp.float32)
    mask = listed[:, len(steps) - 1 :] > 0
    code = jnp.where(mask, jax.nn.softplus(preacts), 0.0).astype(jnp.bfloat16)
    sigma = jnp.where(mask, jax.nn.sigmoid(preacts), 0.0)
    codes[half], sigmas[half] = lax.optimization_barrier((code, sigma))
    other_codes = to_core(codes[half])

    errors = rebuilt.astype(jnp.float32) + swapped.astype(jnp.float32)
    for code, word in ((codes[half], words[half]), (other_codes, other_words)):
        errors = errors + jnp.einsum("rl,ld->rd", code, word, preferred_element_type=jnp.float32)
    errors = errors.astype(jnp.bfloat16)

    def grads_of(step, token):
        (sigma,) = after((sigmas[step],), token)
        slopes = slope(errors, words[step], sigma)
        return gradient(codes[step], slopes, errors, rows)

    def send(x):
        return x.astype(jnp.bfloat16)

    slopes = jnp.einsum("rd,ld->rl", errors, words[half], preferred_element_type=jnp.float32)
    slopes = lax.optimization_barrier((slopes * sigmas[half]).astype(jnp.bfloat16))
    far = jnp.einsum("rl,rd->ld", codes[half], errors, preferred_element_type=jnp.float32)
    far = send(far + jnp.einsum("rl,rd->ld", slopes, rows, preferred_element_type=jnp.float32))
    up = (to_right(far[:cut]), None)
    down = (None, to_left(far[cut:]))
    tokens = (far, far)
    for step in range(half - 1, 0, -1):
        ahead, behind = grads_of(step, tokens[0]), grads_of(-step, tokens[1])
        tokens = (up[0], down[1])
        up = tuple(to_right(join(ahead, came, k)) for k, came in enumerate(up))
        down = tuple(to_left(join(behind, came, k)) for k, came in enumerate(down))
    mine = grads_of(0, tokens[0])
    for came in (up, down):
        mine = mine + jnp.concatenate(came).astype(jnp.float32)
    return (mine / block_rows).astype(jnp.bfloat16)


def solution(mesh):
    in_specs = (
        P(("grp", "row"), "lat", None),
        P("grp", None),
        P(("grp", "lat", "row"), None),
        P(("grp", "lat", "row")),
        P("grp"),
    )
    out_specs = P(("grp", "lat", "row"), None)
    lat_count, row_count = mesh.shape["lat"], mesh.shape["row"]

    def body(activations, act_blocks, dictionary, enc_bias, dec_bias):
        gathered = lat_count * dictionary.size * dictionary.dtype.itemsize
        fits = row_count == 2 and lat_count % 2 == 0 and gathered <= GATHER_LIMIT
        step = ring_body if fits else exchange_body
        return step(activations, act_blocks, dictionary, enc_bias, dec_bias)

    return jax.shard_map(body, mesh=mesh, in_specs=in_specs, out_specs=out_specs, check_vma=False)
```
